512 devices in a mesh: section: 4 (over y), lane: 16 (over z), group: 8 (over x, core).
Axes of the slice: x: 4, y: 4, z: 16, core: 2. Of those that a mesh axis runs over, the one named last changes fastest.
Arguments:
- raw: bfloat16 [65536, 3072], P(('section', 'lane'), 'group'), may hold values from -6 to 6
- taps: float32 [64], replicated, may hold values from -0.75 to 0.75
- whitening: bfloat16 [3072, 384], P('group'), may hold values from -0.3125 to 0.3125
- basis: bfloat16 [121, 6], replicated, may hold values from -0.5 to 0.5
- project: bfloat16 [2304, 384], replicated, may hold values from -0.125 to 0.125
- centroids: bfloat16 [8, 1024, 384], P('group'), may hold values from -40 to 40
- prior: float32 [8, 1024], P('group', 'lane'), may hold values from 0.25 to 4
- times: int32 [64, 8, 128], P(('section', 'lane'), 'group'), may hold values from 0 to 1023, as said below
- counts: int32 [64, 8], P(('section', 'lane'), 'group'), may hold values from 64 to 128
Outputs:
- snapshots: float32 [4, 8, 1024, 384], P('section', 'group', 'lane')
The draws below stay inside these ranges and needn't reach their ends.
Inputs may be any that keep to these rules, and one draw needn't show every extreme that they name: Within each segment and probe the times do not fall.
All inputs are finite; a program needn't handle non-finite values.
Results may differ from the reference program's by a relative error of at most 0.0085.
Values may be sent and summed in bfloat16 or wider, within the bound.
No kernel may reach another device: no remote copies, remote signals or barrier semaphores. Data moves between devices by JAX's collectives and lax.ppermute only.
A program may use at most 64 MiB of HBM per device.

```python
import math
import jax
import jax.numpy as jnp
from jax import lax

CH = 384
F = 384
TAPS = 64
SNIP = 121
RANKS = 6
SEG = 1024
SPK = 128
HALF = 60
CHANNELS = 3072
SEGMENTS = 64
TIME = 65536
CG = 1024
CENTROIDS = 8192
N_SECTION = 4
N_LANE = 16
N_GROUP = 8


def draw_centroids(key, part):
    base = jnp.clip(jax.random.normal(key, (N_GROUP, CG, F), jnp.float32), -6.0, 6.0)
    signs = jnp.where(jax.random.bernoulli(jax.random.fold_in(key, 11), 0.5, (F,)), 1.0, -1.0).astype(jnp.float32)
    common = 32.0 * signs
    return (base + common[None, None, :]).astype(jnp.bfloat16)


def draw_times(key, part):
    drawn = jax.random.randint(key, (SEGMENTS, N_GROUP, SPK), 0, SEG, dtype=jnp.int32)
    ordered = jnp.sort(drawn, axis=-1)
    lowest = jnp.zeros((SEGMENTS, N_GROUP, 1), jnp.int32)
    highest = jnp.full((SEGMENTS, N_GROUP, 1), SEG - 1, jnp.int32)
    return jnp.concatenate([lowest, ordered[:, :, 1:SPK - 1], highest], axis=-1)


def draw_counts(key, part):
    drawn = jax.random.randint(key, (SEGMENTS, N_GROUP), SPK // 2, SPK + 1, dtype=jnp.int32)
    full_row = jnp.full((SEGMENTS, 1), SPK, jnp.int32)
    return jnp.concatenate([full_row, drawn[:, 1:]], axis=1)


def steps_of(own_key, extent, pieces, low, high):
    gain = 1.0
    for axis_at, parts in pieces:
        heights = jax.random.uniform(jax.random.fold_in(jax.random.fold_in(own_key, 6), axis_at), (parts,), jnp.float32, low / len(pieces), high / len(pieces))
        gain = gain * jnp.repeat(jnp.exp(heights), extent[axis_at] // parts).reshape((-1,) + (1,) * (len(extent) - 1 - axis_at))
    return gain


def gaussian(own_key, dims, scale, reach, shards=(), held_as=jnp.bfloat16):
    values = jax.random.normal(own_key, dims, jnp.float32) * scale
    if len(shards) > 0:
        values = steps_of(own_key, dims, shards, -0.22, 0.18) * values
    return jnp.clip(values, min=-reach, max=reach).astype(held_as)


def setup_inputs(seed: int = 0) -> dict:
    seeds = jax.random.split(jax.random.key(seed), 10)
    return {
        "raw": gaussian(seeds[0], (TIME, CHANNELS), 1.0, 6.0, ((0, 64), (1, 8))),
        "taps": gaussian(seeds[1], (TAPS,), TAPS ** -0.5, 0.75, (), jnp.float32),
        "whitening": gaussian(seeds[2], (CHANNELS, CH), CH ** -0.5, 0.3125, ((0, 8),)),
        "basis": gaussian(seeds[3], (SNIP, RANKS), SNIP ** -0.5, 0.5),
        "project": gaussian(seeds[4], (RANKS * CH, F), (RANKS * CH) ** -0.5, 0.125),
        "centroids": draw_centroids(jax.random.fold_in(seeds[9], 71), 0),
        "prior": jnp.clip(jnp.exp(math.log(4.0) - 2.7725887 * jax.random.uniform(seeds[6], (N_GROUP, CG), jnp.float32) ** steps_of(seeds[6], (N_GROUP, CG), ((0, 8), (1, 16)), -0.2, 0.2)), 0.25, 4.0),
        "times": draw_times(jax.random.fold_in(seeds[9], 71), 0),
        "counts": draw_counts(jax.random.fold_in(seeds[9], 71), 0),
    }


sharpness = 0.25


def run_filter(extended, taps, out_rows):
    num_taps = taps.shape[0]
    total = jnp.zeros((out_rows, extended.shape[1]), jnp.float32)
    for tap_index in range(num_taps):
        start = num_taps - 1 - tap_index
        total = total + taps[tap_index] * extended[start:start + out_rows].astype(jnp.float32)
    return total


def probe_features(inputs, taps, basis, project):
    raw_probe, white_matrix, probe_times = inputs
    extended = jnp.concatenate([jnp.zeros((TAPS - 1, CH), jnp.bfloat16), raw_probe], axis=0)
    trace = run_filter(extended, taps, TIME).astype(jnp.bfloat16)
    white = jnp.dot(trace, white_matrix, preferred_element_type=jnp.float32).astype(jnp.bfloat16)
    padded = jnp.concatenate([jnp.zeros((HALF, CH), jnp.bfloat16), white, jnp.zeros((HALF, CH), jnp.bfloat16)], axis=0)

    def segment_features(segment_inputs):
        seg_index, seg_times = segment_inputs
        starts = (seg_index * SEG + seg_times).astype(jnp.int32)
        snippets = jax.vmap(lambda begin: lax.dynamic_slice_in_dim(padded, begin, SNIP, 0))(starts)
        comps = jnp.einsum("svc,vr->src", snippets.astype(jnp.float32), basis.astype(jnp.float32)).astype(jnp.bfloat16)
        flat = comps.reshape(comps.shape[0], RANKS * CH)
        return jnp.dot(flat, project, preferred_element_type=jnp.float32).astype(jnp.bfloat16)

    return lax.map(segment_features, (jnp.arange(SEGMENTS, dtype=jnp.int32), probe_times))


def reference(raw, taps, whitening, basis, project, centroids, prior, times, counts):
    raw_groups = raw.reshape(TIME, N_GROUP, CH).transpose(1, 0, 2)
    white_groups = whitening.reshape(N_GROUP, CH, CH)
    time_groups = times.transpose(1, 0, 2)
    feats = lax.map(lambda inputs: probe_features(inputs, taps, basis, project), (raw_groups, white_groups, time_groups))
    centers = centroids.reshape(CENTROIDS, F)
    prior_flat = prior.reshape(CENTROIDS)

    def lane_step(carry, seg_index):
        spikes = lax.dynamic_index_in_dim(feats, seg_index, 1, keepdims=False).reshape(N_GROUP * SPK, F)
        live_count = lax.dynamic_index_in_dim(counts, seg_index, 0, keepdims=False)
        live_rows = (jnp.arange(SPK, dtype=jnp.int32)[None, :] < live_count[:, None]).reshape(N_GROUP * SPK)
        logits = lax.dot_general(spikes, centers, (((1,), (1,)), ((), ())), preferred_element_type=jnp.float32) * sharpness
        top = jnp.max(logits, axis=1)
        lse = top + jnp.log(jnp.sum(jnp.exp(logits - top[:, None]), axis=1))
        resp = (jnp.exp(logits - lse[:, None]) * live_rows.astype(jnp.float32)[:, None]).astype(jnp.bfloat16)
        sums = lax.dot_general(resp, spikes, (((0,), (0,)), ((), ())), preferred_element_type=jnp.float32)
        mass = jnp.sum(resp.astype(jnp.float32), axis=0)
        return (carry[0] + sums, carry[1] + mass), None

    carry = (jnp.zeros((CENTROIDS, F), jnp.float32), jnp.zeros((CENTROIDS,), jnp.float32))
    frames = []
    for section_index in range(N_SECTION):
        seg_ids = jnp.arange(section_index * N_LANE, (section_index + 1) * N_LANE, dtype=jnp.int32)
        carry, unused = lax.scan(lane_step, carry, seg_ids)
        numer = prior_flat[:, None] * centers.astype(jnp.float32) + carry[0]
        snap = numer / (prior_flat + carry[1])[:, None]
        frames.append(snap.reshape(N_GROUP, CG, F))
    return jnp.stack(frames, axis=0)
```

```python
import functools
import math

import jax
import jax.numpy as jnp
from jax import lax
from jax.experimental import pallas as pl
from jax.experimental.pallas import tpu as pltpu
from jax.sharding import PartitionSpec as P

F32 = jnp.float32
BF16 = jnp.bfloat16
LOG2E = math.log2(math.e)
SHARPNESS = 0.25
DEAD = 1e30

SEG = 1024
CH = 384
FEAT = 384
SPK = 128
TAPS = 64
SNIP = 121
HALF = 60
RANKS = 6
GROUP = 8
LANES = 16
SECTIONS = 4
NEAR = 4
FAR = 4
CG = 1024
ROWS = 64
BEFORE = 128
AFTER = 64
BLOCK = 192
SPAN = BLOCK + TAPS
WHITE_ROWS = 1152
PLACE = 1280
PAY = 208
SUM_ROWS = 192
VMEM_LIMIT = 56 * 1024 * 1024

VMEM = pl.BlockSpec(memory_space=pltpu.VMEM)
SMEM = pl.BlockSpec(memory_space=pltpu.SMEM)
ANY = pl.BlockSpec(memory_space=pl.ANY)


def call(kernel, out_shape, in_specs, out_specs, scratch=(), flops=0, moved=0):
    return pl.pallas_call(
        kernel,
        out_shape=out_shape,
        in_specs=in_specs,
        out_specs=out_specs,
        scratch_shapes=list(scratch),
        compiler_params=pltpu.CompilerParams(vmem_limit_bytes=VMEM_LIMIT),
        cost_estimate=pl.CostEstimate(flops=flops, bytes_accessed=moved, transcendentals=0),
    )


def features_kernel(
    before, after, raw, taps, whitening, basis, project, times, out,
    window, band, row, snip, white, place, comps, flat, held, raw_sem, project_sem,
):
    raw_copy = pltpu.make_async_copy(raw, window.at[pl.ds(BEFORE, SEG)], raw_sem)
    raw_copy.start()
    project_copy = pltpu.make_async_copy(project, held, project_sem)
    project_copy.start()

    row[...] = jnp.zeros_like(row)
    row[0:1, 0:TAPS] = taps[...]
    spread = jnp.broadcast_to(row[0:1, :], (SPAN, SPAN))
    shifted = pltpu.roll(spread, SPAN - TAPS, 1, stride=1, stride_axis=0)
    table = jnp.transpose(shifted)[0:BLOCK, :]
    high = table.astype(BF16)
    band[0:BLOCK, :] = high
    band[BLOCK : 2 * BLOCK, :] = (table - high.astype(F32)).astype(BF16)

    snip[...] = jnp.zeros_like(snip)
    snip[0:RANKS, 0:SNIP] = basis[...].astype(F32)

    def clear(i, carry):
        place[pl.ds(pl.multiple_of(i * 32, 32), 32), :] = jnp.zeros((32, PLACE), F32)
        return carry

    lax.fori_loop(0, SPK * 8 // 32, clear, 0)
    shape = snip[...]

    def put(s, carry):
        u = times[0, 0, s] + (64 - HALF)
        start = pl.multiple_of((u >> 7) * 128, 128)
        at = pl.multiple_of(s * 8, 8)
        place[pl.ds(at, 8), pl.ds(start, 256)] = pltpu.roll(shape, u & 127, 1)
        return carry

    lax.fori_loop(0, SPK, put, 0, unroll=8)

    window[0:BEFORE, :] = before[...]
    window[BEFORE + SEG : BEFORE + SEG + AFTER, :] = after[...]
    raw_copy.wait()
    for b in range(WHITE_ROWS // BLOCK):
        rows = window[b * BLOCK : b * BLOCK + SPAN, :]
        both = jnp.dot(band[...], rows, preferred_element_type=F32)
        trace = (both[0:BLOCK] + both[BLOCK : 2 * BLOCK]).astype(BF16)
        white[b * BLOCK : (b + 1) * BLOCK, :] = jnp.dot(
            trace, whitening[...], preferred_element_type=F32
        ).astype(BF16)
    white[WHITE_ROWS:PLACE, :] = jnp.zeros((PLACE - WHITE_ROWS, CH), BF16)
    last = (lax.axis_index("section") == SECTIONS - 1) & (lax.axis_index("lane") == LANES - 1)

    @pl.when(last)
    def _():
        white[64 + SEG : WHITE_ROWS, :] = jnp.zeros((WHITE_ROWS - 64 - SEG, CH), BF16)

    for c in range(4):
        part = place[c * 256 : (c + 1) * 256, :].astype(BF16)
        found = jnp.dot(part, white[...], preferred_element_type=F32)
        for i in range(CH // 128):
            comps[i, c * 256 : (c + 1) * 256, :] = found[:, i * 128 : (i + 1) * 128]
    for r in range(RANKS):
        for i in range(CH // 128):
            flat[:, r * CH + i * 128 : r * CH + (i + 1) * 128] = comps[
                i, pl.ds(r, SPK, stride=8), :
            ].astype(BF16)
    project_copy.wait()
    out[...] = jnp.dot(flat[...], held[...], preferred_element_type=F32).astype(BF16)


def features(before, after, raw, taps, whitening, basis, project, times):
    return call(
        features_kernel,
        jax.ShapeDtypeStruct((SPK, FEAT), BF16),
        [VMEM, VMEM, ANY, VMEM, VMEM, VMEM, ANY, SMEM],
        VMEM,
        [
            pltpu.VMEM((BEFORE + SEG + AFTER, CH), BF16),
            pltpu.VMEM((2 * BLOCK, SPAN), BF16),
            pltpu.VMEM((8, SPAN), F32),
            pltpu.VMEM((8, 256), F32),
            pltpu.VMEM((PLACE, CH), BF16),
            pltpu.VMEM((SPK * 8, PLACE), F32),
            pltpu.VMEM((CH // 128, SPK * 8, 128), F32),
            pltpu.VMEM((SPK, RANKS * CH), BF16),
            pltpu.VMEM((RANKS * CH, FEAT), BF16),
            pltpu.SemaphoreType.DMA,
            pltpu.SemaphoreType.DMA,
        ],
        flops=2_500_000_000,
        moved=4_000_000,
    )(before, after, raw, taps, whitening, basis, project, times)


def scores_kernel(spikes, centers, counts, shares, weights, tops, logits):
    for b in range(4):
        block = spikes[b * 256 : (b + 1) * 256, :]
        top = None
        for k in range(4):
            part = lax.dot_general(
                centers[0, k * 256 : (k + 1) * 256, :],
                block,
                (((1,), (1,)), ((), ())),
                preferred_element_type=F32,
            ) * (SHARPNESS * LOG2E)
            logits[k * 256 : (k + 1) * 256, b * 256 : (b + 1) * 256] = part
            best = jnp.max(part, axis=0, keepdims=True)
            top = best if top is None else jnp.maximum(top, best)
        total = jnp.zeros((1, 256), F32)
        for k in range(4):
            part = jnp.exp2(logits[k * 256 : (k + 1) * 256, b * 256 : (b + 1) * 256] - top)
            total = total + jnp.sum(part, axis=0, keepdims=True)
            weights[k * 256 : (k + 1) * 256, b * 256 : (b + 1) * 256] = part.astype(BF16)
        lse = top + jnp.log2(total)
        for h in range(2):
            g = 2 * b + h
            mine = lse[:, h * 128 : (h + 1) * 128]
            slot = lax.broadcasted_iota(jnp.int32, (1, 128), 1)
            dead = (lax.axis_index("group") == g) & (slot >= counts[0, 0])
            tops[g : g + 1, :] = top[:, h * 128 : (h + 1) * 128]
            shares[:, g, :] = jnp.broadcast_to(jnp.where(dead, DEAD, mine), (GROUP, 128))


def scores(spikes, centers, counts):
    return call(
        scores_kernel,
        (
            jax.ShapeDtypeStruct((GROUP, GROUP, SPK), F32),
            jax.ShapeDtypeStruct((CG, GROUP * SPK), BF16),
            jax.ShapeDtypeStruct((GROUP, SPK), F32),
        ),
        [VMEM, VMEM, SMEM],
        (VMEM, VMEM, VMEM),
        [pltpu.VMEM((CG, GROUP * SPK), F32)],
        flops=1_000_000_000,
        moved=4_000_000,
    )(spikes, centers, counts)


def sums_kernel(shares, weights, tops, spikes, out):
    best = shares[0]
    for g in range(1, GROUP):
        best = jnp.maximum(best, shares[g])
    total = jnp.zeros_like(best)
    for g in range(GROUP):
        total = total + jnp.exp2(shares[g] - best)
    scale = jnp.exp2(tops[...] - best) / total
    ones = jnp.ones((256, 128), BF16)
    row = lax.broadcasted_iota(jnp.int32, (ROWS, 128), 0)
    lane = lax.broadcasted_iota(jnp.int32, (ROWS, 128), 1)
    pick = row == (lane & (ROWS - 1))
    front = lax.broadcasted_iota(jnp.int32, (1, 128), 1) < ROWS
    for k in range(4):
        acc = None
        for b in range(4):
            parts = []
            for h in range(2):
                g = 2 * b + h
                wide = weights[k * 256 : (k + 1) * 256, g * 128 : (g + 1) * 128].astype(F32)
                parts.append((wide * scale[g : g + 1, :]).astype(BF16))
            resp = jnp.concatenate(parts, axis=1)
            rhs = jnp.concatenate([spikes[b * 256 : (b + 1) * 256, :], ones], axis=1)
            term = jnp.dot(resp, rhs, preferred_element_type=F32)
            acc = term if acc is None else acc + term
        for i in range(4):
            owner = 4 * k + i
            far, near = owner // NEAR, owner % NEAR
            rows = acc[i * ROWS : (i + 1) * ROWS, :]
            for c in range(3):
                out[near, far, c * ROWS : (c + 1) * ROWS, :] = rows[
                    :, c * 128 : (c + 1) * 128
                ].astype(BF16)
            mass = jnp.sum(jnp.where(pick, rows[:, 384:512], 0.0), axis=0, keepdims=True)
            out[near, far, SUM_ROWS:PAY, :] = split(mass, front)


def split(mass, front):
    high = mass.astype(BF16).astype(F32)
    return jnp.broadcast_to(
        jnp.where(front, high, mass - high), (PAY - SUM_ROWS, 128)
    ).astype(BF16)


def sums(shares, weights, tops, spikes):
    return call(
        sums_kernel,
        jax.ShapeDtypeStruct((NEAR, FAR, PAY, 128), BF16),
        [VMEM] * 4,
        VMEM,
        flops=1_000_000_000,
        moved=4_000_000,
    )(shares, weights, tops, spikes)


def near_kernel(got, own, one, two, three):
    front = lax.broadcasted_iota(jnp.int32, (1, 128), 1) < ROWS
    mine = lax.axis_index("lane") // NEAR
    for d, out in enumerate((own, one, two, three)):
        far = lax.rem(mine + d, FAR)
        acc = got[0, far].astype(F32)
        for n in range(1, NEAR):
            acc = acc + got[n, far].astype(F32)
        tail = acc[SUM_ROWS : SUM_ROWS + 1, :]
        mass = tail + pltpu.roll(tail, ROWS, 1)
        out[0:SUM_ROWS, :] = acc[0:SUM_ROWS].astype(out.dtype)
        if d == 0:
            out[SUM_ROWS:PAY, :] = jnp.broadcast_to(mass, (PAY - SUM_ROWS, 128))
        else:
            out[SUM_ROWS:PAY, :] = split(mass, front)


def far_kernel(own, one, two, three, out):
    acc = one[...].astype(F32) + two[...].astype(F32) + three[...].astype(F32)
    tail = acc[SUM_ROWS:PAY, :]
    out[0:SUM_ROWS, :] = own[0:SUM_ROWS, :] + acc[0:SUM_ROWS]
    out[SUM_ROWS:PAY, :] = own[SUM_ROWS:PAY, :] + tail + pltpu.roll(tail, ROWS, 1)


def final_kernel(own, one, two, three, centers, prior, out, held, sem):
    lane_at = lax.axis_index("lane")
    copy = pltpu.make_async_copy(
        centers.at[0, pl.ds(pl.multiple_of(lane_at * ROWS, ROWS), ROWS)], held, sem
    )
    copy.start()
    acc = own[...] + one[...] + two[...] + three[...]
    row = lax.broadcasted_iota(jnp.int32, (ROWS, ROWS), 0)
    lane = lax.broadcasted_iota(jnp.int32, (ROWS, ROWS), 1)
    pick = row == lane

    def column(value):
        wide = jnp.broadcast_to(value, (ROWS, ROWS))
        return jnp.sum(jnp.where(pick, wide, 0.0), axis=1, keepdims=True)

    weight = column(prior[...])
    inverse = 1.0 / (weight + column(acc[SUM_ROWS : SUM_ROWS + 1, 0:ROWS]))
    copy.wait()
    for c in range(3):
        numer = weight * held[:, c * 128 : (c + 1) * 128].astype(F32) + acc[
            c * ROWS : (c + 1) * ROWS, :
        ]
        out[0, 0, :, c * 128 : (c + 1) * 128] = numer * inverse


def per_device(raw, taps, whitening, basis, project, centroids, prior, times, counts):
    windows = ("section", "lane")
    count = SECTIONS * LANES
    before = lax.ppermute(raw[SEG - BEFORE :], windows, [(i, i + 1) for i in range(count - 1)])
    after = lax.ppermute(raw[:AFTER], windows, [(i + 1, i) for i in range(count - 1)])
    feats = features(
        before, after, raw, taps.reshape(1, TAPS), whitening, basis.T, project, times
    )
    spikes = lax.all_gather(feats, "group", axis=0, tiled=True)
    shares, weights, tops = scores(spikes, centroids, counts)
    shares = lax.all_to_all(shares, "group", 0, 0)
    parts = sums(shares, weights, tops, spikes)
    near = [[NEAR * far + n for n in range(NEAR)] for far in range(FAR)]
    got = lax.all_to_all(parts, "lane", 0, 0, axis_index_groups=near)
    small = jax.ShapeDtypeStruct((PAY, 128), BF16)
    wide = jax.ShapeDtypeStruct((PAY, 128), F32)
    own, *sent = call(
        near_kernel, (wide, small, small, small), [VMEM], (VMEM,) * 4, moved=1_000_000
    )(got)
    took = [
        lax.ppermute(part, "lane", [(i, (i + NEAR * (d + 1)) % LANES) for i in range(LANES)])
        for d, part in enumerate(sent)
    ]
    total = call(far_kernel, wide, [VMEM] * 4, VMEM, moved=300_000)(own, *took)
    earlier = [
        lax.ppermute(total, "section", [(i, i + d) for i in range(SECTIONS - d)])
        for d in range(1, SECTIONS)
    ]
    return call(
        final_kernel,
        jax.ShapeDtypeStruct((1, 1, ROWS, FEAT), F32),
        [VMEM, VMEM, VMEM, VMEM, ANY, VMEM],
        VMEM,
        [pltpu.VMEM((ROWS, FEAT), BF16), pltpu.SemaphoreType.DMA],
        moved=600_000,
    )(total, *earlier, centroids, prior)


def solution(mesh):
    placed = (
        P(("section", "lane"), "group"),
        P(),
        P("group", None),
        P(),
        P(),
        P("group", None, None),
        P("group", "lane"),
        P(("section", "lane"), "group", None),
        P(("section", "lane"), "group"),
    )
    return jax.shard_map(
        per_device,
        mesh=mesh,
        in_specs=placed,
        out_specs=P("section", "group", "lane", None),
        check_vma=False,
    )
```

```python
import functools
import math

import jax
import jax.numpy as jnp
from jax import lax
from jax.experimental import pallas as pl
from jax.experimental.pallas import tpu as pltpu
from jax.sharding import PartitionSpec as P

F32 = jnp.float32
BF16 = jnp.bfloat16
LOG2E = math.log2(math.e)
SHARPNESS = 0.25
DEAD = 1e30

SEG = 1024
CH = 384
FEAT = 384
SPK = 128
TAPS = 64
SNIP = 121
HALF = 60
RANKS = 6
GROUP = 8
LANES = 16
SECTIONS = 4
NEAR = 4
FAR = 4
CG = 1024
ROWS = 64
BEFORE = 128
AFTER = 64
BLOCK = 192
SPAN = BLOCK + TAPS
PLACE = 1280
HEAD = 128
LATE = 1024
MIDDLE = 960
EDGE = HEAD + PLACE - LATE
PAY = 208
SUM_ROWS = 192
VMEM_LIMIT = 20 * 1024 * 1024

VMEM = pl.BlockSpec(memory_space=pltpu.VMEM)
SMEM = pl.BlockSpec(memory_space=pltpu.SMEM)
ANY = pl.BlockSpec(memory_space=pl.ANY)


def call(kernel, out_shape, in_specs, out_specs, scratch=(), flops=0, moved=0):
    return pl.pallas_call(
        kernel,
        out_shape=out_shape,
        in_specs=in_specs,
        out_specs=out_specs,
        scratch_shapes=list(scratch),
        compiler_params=pltpu.CompilerParams(vmem_limit_bytes=VMEM_LIMIT),
        cost_estimate=pl.CostEstimate(flops=flops, bytes_accessed=moved, transcendentals=0),
    )


def inner_kernel(
    raw, taps, whitening, basis, times, found, middle, place, band,
    row, snip, rows,
):
    row[...] = jnp.zeros_like(row)
    row[0:1, 0:TAPS] = taps[...]
    spread = jnp.broadcast_to(row[0:1, :], (SPAN, SPAN))
    shifted = pltpu.roll(spread, SPAN - TAPS, 1, stride=1, stride_axis=0)
    table = jnp.transpose(shifted)[0:BLOCK, :]
    high = table.astype(BF16)
    band[0:BLOCK, :] = high
    band[BLOCK : 2 * BLOCK, :] = (table - high.astype(F32)).astype(BF16)

    snip[...] = jnp.zeros_like(snip)
    snip[0:RANKS, 0:SNIP] = basis[...].astype(F32)
    shape = snip[...]
    rows[...] = jnp.zeros_like(rows)

    def put(s, carry):
        u = times[0, 0, s] + (64 - HALF)
        start = pl.multiple_of((u >> 7) * 128, 128)
        at = pl.multiple_of(s * 8, 8)
        rows[pl.ds(at, 8), pl.ds(start, 256)] = pltpu.roll(shape, u & 127, 1)
        return carry

    lax.fori_loop(0, SPK, put, 0, unroll=8)

    for b in range(5):
        both = jnp.dot(
            band[...], raw[b * BLOCK : b * BLOCK + SPAN, :], preferred_element_type=F32
        )
        trace = (both[0:BLOCK] + both[BLOCK : 2 * BLOCK]).astype(BF16)
        middle[b * BLOCK : (b + 1) * BLOCK, :] = jnp.dot(
            trace, whitening[...], preferred_element_type=F32
        ).astype(BF16)
    for c in range(4):
        part = slice(c * 256, (c + 1) * 256)
        place[part, 0:HEAD] = rows[part, 0:HEAD].astype(BF16)
        place[part, HEAD:EDGE] = rows[part, LATE:PLACE].astype(BF16)
        found[part, :] = jnp.dot(
            rows[part, HEAD:LATE].astype(BF16), middle[0 : LATE - HEAD, :],
            preferred_element_type=F32,
        )


def inner(raw, taps, whitening, basis, times):
    return call(
        inner_kernel,
        (
            jax.ShapeDtypeStruct((SPK * 8, CH), F32),
            jax.ShapeDtypeStruct((MIDDLE, CH), BF16),
            jax.ShapeDtypeStruct((SPK * 8, EDGE), BF16),
            jax.ShapeDtypeStruct((2 * BLOCK, SPAN), BF16),
        ),
        [VMEM, VMEM, VMEM, VMEM, SMEM],
        (VMEM, VMEM, VMEM, VMEM),
        [
            pltpu.VMEM((8, SPAN), F32),
            pltpu.VMEM((8, 256), F32),
            pltpu.VMEM((SPK * 8, PLACE), F32),
        ],
        flops=2_000_000_000,
        moved=6_000_000,
    )(raw, taps, whitening, basis, times)


def features_kernel(
    before, after, raw, whitening, found, middle, place, band, project, out,
    window, white, comps, flat,
):
    window[0:BEFORE, :] = before[...]
    window[BEFORE:SPAN, :] = raw[0 : SPAN - BEFORE, :]
    window[SPAN : 2 * SPAN - AFTER, :] = raw[SEG - SPAN + AFTER : SEG, :]
    window[2 * SPAN - AFTER : 2 * SPAN, :] = after[...]
    for b in range(2):
        both = jnp.dot(band[...], window[b * SPAN : (b + 1) * SPAN, :], preferred_element_type=F32)
        trace = (both[0:BLOCK] + both[BLOCK : 2 * BLOCK]).astype(BF16)
        fresh = jnp.dot(trace, whitening[...], preferred_element_type=F32).astype(BF16)
        if b == 0:
            white[0:HEAD, :] = fresh[0:HEAD]
        else:
            white[HEAD + 64 : HEAD + 128, :] = fresh[BLOCK - 64 : BLOCK]
    white[HEAD : HEAD + 64, :] = middle[LATE - HEAD : MIDDLE, :]
    white[HEAD + 128 : EDGE, :] = jnp.zeros((EDGE - HEAD - 128, CH), BF16)
    last = (lax.axis_index("section") == SECTIONS - 1) & (lax.axis_index("lane") == LANES - 1)

    @pl.when(last)
    def _():
        white[HEAD + 64 : HEAD + 128, :] = jnp.zeros((64, CH), BF16)

    for c in range(4):
        part = slice(c * 256, (c + 1) * 256)
        whole = found[part, :] + jnp.dot(place[part, :], white[...], preferred_element_type=F32)
        for i in range(CH // 128):
            comps[i, part, :] = whole[:, i * 128 : (i + 1) * 128]
    for r in range(RANKS):
        for i in range(CH // 128):
            flat[:, r * CH + i * 128 : r * CH + (i + 1) * 128] = comps[
                i, pl.ds(r, SPK, stride=8), :
            ].astype(BF16)
    out[...] = jnp.dot(flat[...], project[...], preferred_element_type=F32).astype(BF16)


def features(before, after, raw, whitening, found, middle, place, band, project):
    return call(
        features_kernel,
        jax.ShapeDtypeStruct((SPK, FEAT), BF16),
        [VMEM] * 9,
        VMEM,
        [
            pltpu.VMEM((2 * SPAN, CH), BF16),
            pltpu.VMEM((EDGE, CH), BF16),
            pltpu.VMEM((CH // 128, SPK * 8, 128), F32),
            pltpu.VMEM((SPK, RANKS * CH), BF16),
        ],
        flops=1_000_000_000,
        moved=6_000_000,
    )(before, after, raw, whitening, found, middle, place, band, project)


def scores_kernel(spikes, centers, counts, shares, weights, tops, logits):
    for b in range(4):
        block = spikes[b * 256 : (b + 1) * 256, :]
        top = None
        for k in range(4):
            part = lax.dot_general(
                centers[0, k * 256 : (k + 1) * 256, :],
                block,
                (((1,), (1,)), ((), ())),
                preferred_element_type=F32,
            ) * (SHARPNESS * LOG2E)
            logits[k * 256 : (k + 1) * 256, b * 256 : (b + 1) * 256] = part
            best = jnp.max(part, axis=0, keepdims=True)
            top = best if top is None else jnp.maximum(top, best)
        total = jnp.zeros((1, 256), F32)
        for k in range(4):
            part = jnp.exp2(logits[k * 256 : (k + 1) * 256, b * 256 : (b + 1) * 256] - top)
            total = total + jnp.sum(part, axis=0, keepdims=True)
            weights[k * 256 : (k + 1) * 256, b * 256 : (b + 1) * 256] = part.astype(BF16)
        lse = top + jnp.log2(total)
        for h in range(2):
            g = 2 * b + h
            mine = lse[:, h * 128 : (h + 1) * 128]
            slot = lax.broadcasted_iota(jnp.int32, (1, 128), 1)
            dead = (lax.axis_index("group") == g) & (slot >= counts[0, 0])
            tops[g : g + 1, :] = top[:, h * 128 : (h + 1) * 128]
            shares[:, g, :] = jnp.broadcast_to(jnp.where(dead, DEAD, mine), (GROUP, 128))


def scores(spikes, centers, counts):
    return call(
        scores_kernel,
        (
            jax.ShapeDtypeStruct((GROUP, GROUP, SPK), F32),
            jax.ShapeDtypeStruct((CG, GROUP * SPK), BF16),
            jax.ShapeDtypeStruct((GROUP, SPK), F32),
        ),
        [VMEM, VMEM, SMEM],
        (VMEM, VMEM, VMEM),
        [pltpu.VMEM((CG, GROUP * SPK), F32)],
        flops=1_000_000_000,
        moved=4_000_000,
    )(spikes, centers, counts)


def sums_kernel(shares, weights, tops, spikes, out):
    best = shares[0]
    for g in range(1, GROUP):
        best = jnp.maximum(best, shares[g])
    total = jnp.zeros_like(best)
    for g in range(GROUP):
        total = total + jnp.exp2(shares[g] - best)
    scale = jnp.exp2(tops[...] - best) / total
    ones = jnp.ones((256, 128), BF16)
    row = lax.broadcasted_iota(jnp.int32, (ROWS, 128), 0)
    lane = lax.broadcasted_iota(jnp.int32, (ROWS, 128), 1)
    pick = row == (lane & (ROWS - 1))
    front = lax.broadcasted_iota(jnp.int32, (1, 128), 1) < ROWS
    for k in range(4):
        acc = None
        for b in range(4):
            parts = []
            for h in range(2):
                g = 2 * b + h
                wide = weights[k * 256 : (k + 1) * 256, g * 128 : (g + 1) * 128].astype(F32)
                parts.append((wide * scale[g : g + 1, :]).astype(BF16))
            resp = jnp.concatenate(parts, axis=1)
            rhs = jnp.concatenate([spikes[b * 256 : (b + 1) * 256, :], ones], axis=1)
            term = jnp.dot(resp, rhs, preferred_element_type=F32)
            acc = term if acc is None else acc + term
        for i in range(4):
            owner = 4 * k + i
            far, near = owner // NEAR, owner % NEAR
            rows = acc[i * ROWS : (i + 1) * ROWS, :]
            for c in range(3):
                out[near, far, c * ROWS : (c + 1) * ROWS, :] = rows[
                    :, c * 128 : (c + 1) * 128
                ].astype(BF16)
            mass = jnp.sum(jnp.where(pick, rows[:, 384:512], 0.0), axis=0, keepdims=True)
            out[near, far, SUM_ROWS:PAY, :] = split(mass, front)


def split(mass, front):
    high = mass.astype(BF16).astype(F32)
    return jnp.broadcast_to(
        jnp.where(front, high, mass - high), (PAY - SUM_ROWS, 128)
    ).astype(BF16)


def sums(shares, weights, tops, spikes):
    return call(
        sums_kernel,
        jax.ShapeDtypeStruct((NEAR, FAR, PAY, 128), BF16),
        [VMEM] * 4,
        VMEM,
        flops=1_000_000_000,
        moved=4_000_000,
    )(shares, weights, tops, spikes)


def near_kernel(got, own, one, two, three):
    front = lax.broadcasted_iota(jnp.int32, (1, 128), 1) < ROWS
    mine = lax.axis_index("lane") // NEAR
    for d, out in enumerate((own, one, two, three)):
        far = lax.rem(mine + d, FAR)
        acc = got[0, far].astype(F32)
        for n in range(1, NEAR):
            acc = acc + got[n, far].astype(F32)
        tail = acc[SUM_ROWS : SUM_ROWS + 1, :]
        mass = tail + pltpu.roll(tail, ROWS, 1)
        out[0:SUM_ROWS, :] = acc[0:SUM_ROWS].astype(out.dtype)
        if d == 0:
            out[SUM_ROWS:PAY, :] = jnp.broadcast_to(mass, (PAY - SUM_ROWS, 128))
        else:
            out[SUM_ROWS:PAY, :] = split(mass, front)


def far_kernel(own, one, two, three, out):
    acc = one[...].astype(F32) + two[...].astype(F32) + three[...].astype(F32)
    tail = acc[SUM_ROWS:PAY, :]
    out[0:SUM_ROWS, :] = own[0:SUM_ROWS, :] + acc[0:SUM_ROWS]
    out[SUM_ROWS:PAY, :] = own[SUM_ROWS:PAY, :] + tail + pltpu.roll(tail, ROWS, 1)


def final_kernel(own, one, two, three, centers, prior, out, held, sem):
    lane_at = lax.axis_index("lane")
    copy = pltpu.make_async_copy(
        centers.at[0, pl.ds(pl.multiple_of(lane_at * ROWS, ROWS), ROWS)], held, sem
    )
    copy.start()
    acc = own[...] + one[...] + two[...] + three[...]
    row = lax.broadcasted_iota(jnp.int32, (ROWS, ROWS), 0)
    lane = lax.broadcasted_iota(jnp.int32, (ROWS, ROWS), 1)
    pick = row == lane

    def column(value):
        wide = jnp.broadcast_to(value, (ROWS, ROWS))
        return jnp.sum(jnp.where(pick, wide, 0.0), axis=1, keepdims=True)

    weight = column(prior[...])
    inverse = 1.0 / (weight + column(acc[SUM_ROWS : SUM_ROWS + 1, 0:ROWS]))
    copy.wait()
    for c in range(3):
        numer = weight * held[:, c * 128 : (c + 1) * 128].astype(F32) + acc[
            c * ROWS : (c + 1) * ROWS, :
        ]
        out[0, 0, :, c * 128 : (c + 1) * 128] = numer * inverse


def per_device(raw, taps, whitening, basis, project, centroids, prior, times, counts):
    windows = ("section", "lane")
    count = SECTIONS * LANES
    before = lax.ppermute(raw[SEG - BEFORE :], windows, [(i, i + 1) for i in range(count - 1)])
    after = lax.ppermute(raw[:AFTER], windows, [(i + 1, i) for i in range(count - 1)])
    held = inner(raw, taps.reshape(1, TAPS), whitening, basis.T, times)
    feats = features(before, after, raw, whitening, *held, project)
    spikes = lax.all_gather(feats, "group", axis=0, tiled=True)
    shares, weights, tops = scores(spikes, centroids, counts)
    shares = lax.all_to_all(shares, "group", 0, 0)
    parts = sums(shares, weights, tops, spikes)
    near = [[NEAR * far + n for n in range(NEAR)] for far in range(FAR)]
    got = lax.all_to_all(parts, "lane", 0, 0, axis_index_groups=near)
    small = jax.ShapeDtypeStruct((PAY, 128), BF16)
    wide = jax.ShapeDtypeStruct((PAY, 128), F32)
    own, *sent = call(
        near_kernel, (wide, small, small, small), [VMEM], (VMEM,) * 4, moved=1_000_000
    )(got)
    took = [
        lax.ppermute(part, "lane", [(i, (i + NEAR * (d + 1)) % LANES) for i in range(LANES)])
        for d, part in enumerate(sent)
    ]
    total = call(far_kernel, wide, [VMEM] * 4, VMEM, moved=300_000)(own, *took)
    earlier = [
        lax.ppermute(total, "section", [(i, i + d) for i in range(SECTIONS - d)])
        for d in range(1, SECTIONS)
    ]
    return call(
        final_kernel,
        jax.ShapeDtypeStruct((1, 1, ROWS, FEAT), F32),
        [VMEM, VMEM, VMEM, VMEM, ANY, VMEM],
        VMEM,
        [pltpu.VMEM((ROWS, FEAT), BF16), pltpu.SemaphoreType.DMA],
        moved=600_000,
    )(total, *earlier, centroids, prior)


def solution(mesh):
    placed = (
        P(("section", "lane"), "group"),
        P(),
        P("group", None),
        P(),
        P(),
        P("group", None, None),
        P("group", "lane"),
        P(("section", "lane"), "group", None),
        P(("section", "lane"), "group"),
    )
    return jax.shard_map(
        per_device,
        mesh=mesh,
        in_specs=placed,
        out_specs=P("section", "group", "lane", None),
        check_vma=False,
    )
```

```python
import functools
import math

import jax
import jax.numpy as jnp
from jax import lax
from jax.experimental import pallas as pl
from jax.experimental.pallas import tpu as pltpu
from jax.sharding import PartitionSpec as P

F32 = jnp.float32
BF16 = jnp.bfloat16
LOG2E = math.log2(math.e)
SHARPNESS = 0.25
DEAD = 1e30

SEG = 1024
CH = 384
FEAT = 384
SPK = 128
TAPS = 64
SNIP = 121
HALF = 60
RANKS = 6
GROUP = 8
LANES = 16
SECTIONS = 4
NEAR = 4
FAR = 4
CG = 1024
ROWS = 64
BEFORE = 128
AFTER = 64
BLOCK = 192
SPAN = BLOCK + TAPS
PLACE = 1280
HEAD = 128
LATE = 1024
MIDDLE = 960
EDGE = HEAD + PLACE - LATE
PAY = 208
SUM_ROWS = 192
NEAR_ROWS = FAR * SUM_ROWS + 16
VMEM_LIMIT = 20 * 1024 * 1024

VMEM = pl.BlockSpec(memory_space=pltpu.VMEM)
SMEM = pl.BlockSpec(memory_space=pltpu.SMEM)
ANY = pl.BlockSpec(memory_space=pl.ANY)


def call(kernel, out_shape, in_specs, out_specs, scratch=(), flops=0, moved=0):
    return pl.pallas_call(
        kernel,
        out_shape=out_shape,
        in_specs=in_specs,
        out_specs=out_specs,
        scratch_shapes=list(scratch),
        compiler_params=pltpu.CompilerParams(vmem_limit_bytes=VMEM_LIMIT),
        cost_estimate=pl.CostEstimate(flops=flops, bytes_accessed=moved, transcendentals=0),
    )


def edges_kernel(raw, head, tail):
    head[...] = raw[0:AFTER, :]
    tail[...] = raw[SEG - BEFORE : SEG, :]


def inner_kernel(
    raw, taps, whitening, basis, times, found, middle, place, band,
    row, snip, rows,
):
    row[...] = jnp.zeros_like(row)
    row[0:1, 0:TAPS] = taps[...]
    spread = jnp.broadcast_to(row[0:1, :], (SPAN, SPAN))
    shifted = pltpu.roll(spread, SPAN - TAPS, 1, stride=1, stride_axis=0)
    table = jnp.transpose(shifted)[0:BLOCK, :]
    high = table.astype(BF16)
    band[0:BLOCK, :] = high
    band[BLOCK : 2 * BLOCK, :] = (table - high.astype(F32)).astype(BF16)

    snip[...] = jnp.zeros_like(snip)
    snip[0:RANKS, 0:SNIP] = basis[...].astype(F32)
    shape = snip[...]
    rows[...] = jnp.zeros_like(rows)

    def put(s, carry):
        u = times[0, 0, s] + (64 - HALF)
        start = pl.multiple_of((u >> 7) * 128, 128)
        at = pl.multiple_of(s * 8, 8)
        rows[pl.ds(at, 8), pl.ds(start, 256)] = pltpu.roll(shape, u & 127, 1)
        return carry

    lax.fori_loop(0, SPK, put, 0, unroll=8)

    for b in range(5):
        both = jnp.dot(
            band[...], raw[b * BLOCK : b * BLOCK + SPAN, :], preferred_element_type=F32
        )
        trace = (both[0:BLOCK] + both[BLOCK : 2 * BLOCK]).astype(BF16)
        middle[b * BLOCK : (b + 1) * BLOCK, :] = jnp.dot(
            trace, whitening[...], preferred_element_type=F32
        ).astype(BF16)
    for c in range(4):
        part = slice(c * 256, (c + 1) * 256)
        place[part, 0:HEAD] = rows[part, 0:HEAD].astype(BF16)
        place[part, HEAD:EDGE] = rows[part, LATE:PLACE].astype(BF16)
        found[part, :] = jnp.dot(
            rows[part, HEAD:LATE].astype(BF16), middle[0 : LATE - HEAD, :],
            preferred_element_type=F32,
        )


def inner(raw, taps, whitening, basis, times):
    return call(
        inner_kernel,
        (
            jax.ShapeDtypeStruct((SPK * 8, CH), F32),
            jax.ShapeDtypeStruct((MIDDLE, CH), BF16),
            jax.ShapeDtypeStruct((SPK * 8, EDGE), BF16),
            jax.ShapeDtypeStruct((2 * BLOCK, SPAN), BF16),
        ),
        [VMEM, VMEM, VMEM, VMEM, SMEM],
        (VMEM, VMEM, VMEM, VMEM),
        [
            pltpu.VMEM((8, SPAN), F32),
            pltpu.VMEM((8, 256), F32),
            pltpu.VMEM((SPK * 8, PLACE), F32),
        ],
        flops=2_000_000_000,
        moved=6_000_000,
    )(raw, taps, whitening, basis, times)


def features_kernel(
    before, after, raw, whitening, found, middle, place, band, project, out,
    window, white, comps, flat,
):
    window[0:BEFORE, :] = before[...]
    window[BEFORE:SPAN, :] = raw[0 : SPAN - BEFORE, :]
    window[SPAN : 2 * SPAN - AFTER, :] = raw[SEG - SPAN + AFTER : SEG, :]
    window[2 * SPAN - AFTER : 2 * SPAN, :] = after[...]
    for b in range(2):
        both = jnp.dot(band[...], window[b * SPAN : (b + 1) * SPAN, :], preferred_element_type=F32)
        trace = (both[0:BLOCK] + both[BLOCK : 2 * BLOCK]).astype(BF16)
        fresh = jnp.dot(trace, whitening[...], preferred_element_type=F32).astype(BF16)
        if b == 0:
            white[0:HEAD, :] = fresh[0:HEAD]
        else:
            white[HEAD + 64 : HEAD + 128, :] = fresh[BLOCK - 64 : BLOCK]
    white[HEAD : HEAD + 64, :] = middle[LATE - HEAD : MIDDLE, :]
    white[HEAD + 128 : EDGE, :] = jnp.zeros((EDGE - HEAD - 128, CH), BF16)
    last = (lax.axis_index("section") == SECTIONS - 1) & (lax.axis_index("lane") == LANES - 1)

    @pl.when(last)
    def _():
        white[HEAD + 64 : HEAD + 128, :] = jnp.zeros((64, CH), BF16)

    for c in range(4):
        part = slice(c * 256, (c + 1) * 256)
        whole = found[part, :] + jnp.dot(place[part, :], white[...], preferred_element_type=F32)
        for i in range(CH // 128):
            comps[i, part, :] = whole[:, i * 128 : (i + 1) * 128]
    for r in range(RANKS):
        for i in range(CH // 128):
            flat[:, r * CH + i * 128 : r * CH + (i + 1) * 128] = comps[
                i, pl.ds(r, SPK, stride=8), :
            ].astype(BF16)
    out[...] = jnp.dot(flat[...], project[...], preferred_element_type=F32).astype(BF16)


def features(before, after, raw, whitening, found, middle, place, band, project):
    return call(
        features_kernel,
        jax.ShapeDtypeStruct((SPK, FEAT), BF16),
        [VMEM] * 9,
        VMEM,
        [
            pltpu.VMEM((2 * SPAN, CH), BF16),
            pltpu.VMEM((EDGE, CH), BF16),
            pltpu.VMEM((CH // 128, SPK * 8, 128), F32),
            pltpu.VMEM((SPK, RANKS * CH), BF16),
        ],
        flops=1_000_000_000,
        moved=6_000_000,
    )(before, after, raw, whitening, found, middle, place, band, project)


def scores_kernel(spikes, centers, counts, shares, weights, tops, logits):
    for b in range(4):
        block = spikes[b * 256 : (b + 1) * 256, :]
        top = None
        for k in range(4):
            part = lax.dot_general(
                centers[0, k * 256 : (k + 1) * 256, :],
                block,
                (((1,), (1,)), ((), ())),
                preferred_element_type=F32,
            ) * (SHARPNESS * LOG2E)
            logits[k * 256 : (k + 1) * 256, b * 256 : (b + 1) * 256] = part
            best = jnp.max(part, axis=0, keepdims=True)
            top = best if top is None else jnp.maximum(top, best)
        total = jnp.zeros((1, 256), F32)
        for k in range(4):
            part = jnp.exp2(logits[k * 256 : (k + 1) * 256, b * 256 : (b + 1) * 256] - top)
            total = total + jnp.sum(part, axis=0, keepdims=True)
            weights[k * 256 : (k + 1) * 256, b * 256 : (b + 1) * 256] = part.astype(BF16)
        lse = top + jnp.log2(total)
        for h in range(2):
            g = 2 * b + h
            mine = lse[:, h * 128 : (h + 1) * 128]
            slot = lax.broadcasted_iota(jnp.int32, (1, 128), 1)
            dead = (lax.axis_index("group") == g) & (slot >= counts[0, 0])
            tops[g : g + 1, :] = top[:, h * 128 : (h + 1) * 128]
            shares[:, g, :] = jnp.broadcast_to(jnp.where(dead, DEAD, mine), (GROUP, 128))


def scores(spikes, centers, counts):
    return call(
        scores_kernel,
        (
            jax.ShapeDtypeStruct((GROUP, GROUP, SPK), F32),
            jax.ShapeDtypeStruct((CG, GROUP * SPK), BF16),
            jax.ShapeDtypeStruct((GROUP, SPK), F32),
        ),
        [VMEM, VMEM, SMEM],
        (VMEM, VMEM, VMEM),
        [pltpu.VMEM((CG, GROUP * SPK), F32)],
        flops=1_000_000_000,
        moved=4_000_000,
    )(spikes, centers, counts)


def sums_kernel(shares, weights, tops, spikes, out):
    best = shares[0]
    for g in range(1, GROUP):
        best = jnp.maximum(best, shares[g])
    total = jnp.zeros_like(best)
    for g in range(GROUP):
        total = total + jnp.exp2(shares[g] - best)
    scale = jnp.exp2(tops[...] - best) / total
    ones = jnp.ones((256, 128), BF16)
    row = lax.broadcasted_iota(jnp.int32, (ROWS, 128), 0)
    lane = lax.broadcasted_iota(jnp.int32, (ROWS, 128), 1)
    pick = row == (lane & (ROWS - 1))
    front = lax.broadcasted_iota(jnp.int32, (1, 128), 1) < ROWS
    masses = [[] for _ in range(NEAR)]
    for k in range(4):
        acc = None
        for b in range(4):
            parts = []
            for h in range(2):
                g = 2 * b + h
                wide = weights[k * 256 : (k + 1) * 256, g * 128 : (g + 1) * 128].astype(F32)
                parts.append((wide * scale[g : g + 1, :]).astype(BF16))
            resp = jnp.concatenate(parts, axis=1)
            rhs = jnp.concatenate([spikes[b * 256 : (b + 1) * 256, :], ones], axis=1)
            term = jnp.dot(resp, rhs, preferred_element_type=F32)
            acc = term if acc is None else acc + term
        for i in range(4):
            owner = 4 * k + i
            far, near = owner // NEAR, owner % NEAR
            rows = acc[i * ROWS : (i + 1) * ROWS, :]
            for c in range(3):
                start = far * SUM_ROWS + c * ROWS
                out[near, start : start + ROWS, :] = rows[:, c * 128 : (c + 1) * 128].astype(BF16)
            mass = jnp.sum(jnp.where(pick, rows[:, 384:512], 0.0), axis=0, keepdims=True)
            masses[near].append(mass)
    slot = lax.broadcasted_iota(jnp.int32, (16, 128), 0)
    for near in range(NEAR):
        block = jnp.zeros((16, 128), F32)
        for far in range(FAR):
            block = jnp.where(slot == far, jnp.broadcast_to(masses[near][far], (16, 128)), block)
        high = block.astype(BF16).astype(F32)
        out[near, FAR * SUM_ROWS : NEAR_ROWS, :] = jnp.where(front, high, block - high).astype(BF16)


def split(mass, front):
    high = mass.astype(BF16).astype(F32)
    return jnp.broadcast_to(
        jnp.where(front, high, mass - high), (PAY - SUM_ROWS, 128)
    ).astype(BF16)


def sums(shares, weights, tops, spikes):
    return call(
        sums_kernel,
        jax.ShapeDtypeStruct((NEAR, NEAR_ROWS, 128), BF16),
        [VMEM] * 4,
        VMEM,
        flops=1_000_000_000,
        moved=4_000_000,
    )(shares, weights, tops, spikes)


def near_kernel(got, own, one, two, three):
    front = lax.broadcasted_iota(jnp.int32, (1, 128), 1) < ROWS
    slot = lax.broadcasted_iota(jnp.int32, (16, 128), 0)
    mine = lax.axis_index("lane") // NEAR
    tails = got[0, FAR * SUM_ROWS : NEAR_ROWS, :].astype(F32)
    for n in range(1, NEAR):
        tails = tails + got[n, FAR * SUM_ROWS : NEAR_ROWS, :].astype(F32)
    for d, out in enumerate((own, one, two, three)):
        far = lax.rem(mine + d, FAR)
        part = pl.ds(pl.multiple_of(far * SUM_ROWS, 64), SUM_ROWS)
        acc = got[0, part, :].astype(F32)
        for n in range(1, NEAR):
            acc = acc + got[n, part, :].astype(F32)
        tail = jnp.sum(jnp.where(slot == far, tails, 0.0), axis=0, keepdims=True)
        mass = tail + pltpu.roll(tail, ROWS, 1)
        out[0:SUM_ROWS, :] = acc.astype(out.dtype)
        if d == 0:
            out[SUM_ROWS:PAY, :] = jnp.broadcast_to(mass, (PAY - SUM_ROWS, 128))
        else:
            out[SUM_ROWS:PAY, :] = split(mass, front)


def far_kernel(own, one, two, three, out, sent):
    front = lax.broadcasted_iota(jnp.int32, (1, 128), 1) < ROWS
    acc = one[...].astype(F32) + two[...].astype(F32) + three[...].astype(F32)
    total = own[0:SUM_ROWS, :] + acc[0:SUM_ROWS]
    tail = acc[SUM_ROWS:PAY, :]
    mass = own[SUM_ROWS:PAY, :] + tail + pltpu.roll(tail, ROWS, 1)
    out[0:SUM_ROWS, :] = total
    out[SUM_ROWS:PAY, :] = mass
    sent[0:SUM_ROWS, :] = total.astype(BF16)
    sent[SUM_ROWS:PAY, :] = split(mass[0:1], front)


def final_kernel(own, one, two, three, centers, prior, out, held, sem):
    lane_at = lax.axis_index("lane")
    copy = pltpu.make_async_copy(
        centers.at[0, pl.ds(pl.multiple_of(lane_at * ROWS, ROWS), ROWS)], held, sem
    )
    copy.start()
    past = one[...].astype(F32) + two[...].astype(F32) + three[...].astype(F32)
    acc = own[0:SUM_ROWS, :] + past[0:SUM_ROWS]
    tail = past[SUM_ROWS : SUM_ROWS + 1, :]
    mass = own[SUM_ROWS : SUM_ROWS + 1, :] + tail + pltpu.roll(tail, ROWS, 1)
    row = lax.broadcasted_iota(jnp.int32, (ROWS, ROWS), 0)
    lane = lax.broadcasted_iota(jnp.int32, (ROWS, ROWS), 1)
    pick = row == lane

    def column(value):
        wide = jnp.broadcast_to(value, (ROWS, ROWS))
        return jnp.sum(jnp.where(pick, wide, 0.0), axis=1, keepdims=True)

    weight = column(prior[...])
    inverse = 1.0 / (weight + column(mass[:, 0:ROWS]))
    copy.wait()
    for c in range(3):
        numer = weight * held[:, c * 128 : (c + 1) * 128].astype(F32) + acc[
            c * ROWS : (c + 1) * ROWS, :
        ]
        out[0, 0, :, c * 128 : (c + 1) * 128] = numer * inverse


def per_device(raw, taps, whitening, basis, project, centroids, prior, times, counts):
    windows = ("section", "lane")
    count = SECTIONS * LANES
    head, tail = call(
        edges_kernel,
        (jax.ShapeDtypeStruct((AFTER, CH), BF16), jax.ShapeDtypeStruct((BEFORE, CH), BF16)),
        [VMEM],
        (VMEM, VMEM),
        moved=1_000_000,
    )(raw)
    before = lax.ppermute(tail, windows, [(i, i + 1) for i in range(count - 1)])
    after = lax.ppermute(head, windows, [(i + 1, i) for i in range(count - 1)])
    held = inner(raw, taps.reshape(1, TAPS), whitening, basis.T, times)
    feats = features(before, after, raw, whitening, *held, project)
    spikes = lax.all_gather(feats, "group", axis=0, tiled=True)
    shares, weights, tops = scores(spikes, centroids, counts)
    shares = lax.all_to_all(shares, "group", 0, 0)
    parts = sums(shares, weights, tops, spikes)
    near = [[NEAR * far + n for n in range(NEAR)] for far in range(FAR)]
    got = lax.all_to_all(parts, "lane", 0, 0, axis_index_groups=near)
    small = jax.ShapeDtypeStruct((PAY, 128), BF16)
    wide = jax.ShapeDtypeStruct((PAY, 128), F32)
    own, *sent = call(
        near_kernel, (wide, small, small, small), [VMEM], (VMEM,) * 4, moved=1_000_000
    )(got)
    took = [
        lax.ppermute(part, "lane", [(i, (i + NEAR * (d + 1)) % LANES) for i in range(LANES)])
        for d, part in enumerate(sent)
    ]
    total, sent = call(far_kernel, (wide, small), [VMEM] * 4, (VMEM,) * 2, moved=300_000)(own, *took)
    earlier = [
        lax.ppermute(sent, "section", [(i, i + d) for i in range(SECTIONS - d)])
        for d in range(1, SECTIONS)
    ]
    return call(
        final_kernel,
        jax.ShapeDtypeStruct((1, 1, ROWS, FEAT), F32),
        [VMEM, VMEM, VMEM, VMEM, ANY, VMEM],
        VMEM,
        [pltpu.VMEM((ROWS, FEAT), BF16), pltpu.SemaphoreType.DMA],
        moved=600_000,
    )(total, *earlier, centroids, prior)


def solution(mesh):
    placed = (
        P(("section", "lane"), "group"),
        P(),
        P("group", None),
        P(),
        P(),
        P("group", None, None),
        P("group", "lane"),
        P(("section", "lane"), "group", None),
        P(("section", "lane"), "group"),
    )
    return jax.shard_map(
        per_device,
        mesh=mesh,
        in_specs=placed,
        out_specs=P("section", "group", "lane", None),
        check_vma=False,
    )
```

```python
import functools
import math

import jax
import jax.numpy as jnp
from jax import lax
from jax.experimental import pallas as pl
from jax.experimental.pallas import tpu as pltpu
from jax.sharding import PartitionSpec as P

F32 = jnp.float32
BF16 = jnp.bfloat16
LOG2E = math.log2(math.e)
SHARPNESS = 0.25
DEAD = 1e30

SEG = 1024
CH = 384
FEAT = 384
SPK = 128
TAPS = 64
SNIP = 121
HALF = 60
RANKS = 6
GROUP = 8
LANES = 16
SECTIONS = 4
NEAR = 4
FAR = 4
CG = 1024
ROWS = 64
BEFORE = 128
AFTER = 64
BLOCK = 192
SPAN = BLOCK + TAPS
PLACE = 1280
HEAD = 128
LATE = 1024
MIDDLE = 960
EDGE = HEAD + PLACE - LATE
PAY = 208
SUM_ROWS = 192
NEAR_ROWS = FAR * SUM_ROWS + 16
VMEM_LIMIT = 20 * 1024 * 1024

VMEM = pl.BlockSpec(memory_space=pltpu.VMEM)
SMEM = pl.BlockSpec(memory_space=pltpu.SMEM)
ANY = pl.BlockSpec(memory_space=pl.ANY)


def call(kernel, out_shape, in_specs, out_specs, scratch=(), flops=0, moved=0):
    return pl.pallas_call(
        kernel,
        out_shape=out_shape,
        in_specs=in_specs,
        out_specs=out_specs,
        scratch_shapes=list(scratch),
        compiler_params=pltpu.CompilerParams(vmem_limit_bytes=VMEM_LIMIT),
        cost_estimate=pl.CostEstimate(flops=flops, bytes_accessed=moved, transcendentals=0),
    )


def edges_kernel(raw, head, tail):
    head[...] = raw[0:AFTER, :]
    tail[...] = raw[SEG - BEFORE : SEG, :]


def inner_kernel(
    raw, taps, whitening, basis, times, found, middle, place, band,
    row, snip, rows,
):
    row[...] = jnp.zeros_like(row)
    row[0:1, 0:TAPS] = taps[...]
    spread = jnp.broadcast_to(row[0:1, :], (SPAN, SPAN))
    shifted = pltpu.roll(spread, SPAN - TAPS, 1, stride=1, stride_axis=0)
    table = jnp.transpose(shifted)[0:BLOCK, :]
    high = table.astype(BF16)
    band[0:BLOCK, :] = high
    band[BLOCK : 2 * BLOCK, :] = (table - high.astype(F32)).astype(BF16)

    snip[...] = jnp.zeros_like(snip)
    snip[0:RANKS, 0:SNIP] = basis[...].astype(F32)
    shape = snip[...]
    rows[...] = jnp.zeros_like(rows)

    def put(s, carry):
        u = times[0, 0, s] + (64 - HALF)
        start = pl.multiple_of((u >> 7) * 128, 128)
        at = pl.multiple_of(s * 8, 8)
        rows[pl.ds(at, 8), pl.ds(start, 256)] = pltpu.roll(shape, u & 127, 1)
        return carry

    lax.fori_loop(0, SPK, put, 0, unroll=128)

    for b in range(5):
        both = jnp.dot(
            band[...], raw[b * BLOCK : b * BLOCK + SPAN, :], preferred_element_type=F32
        )
        trace = (both[0:BLOCK] + both[BLOCK : 2 * BLOCK]).astype(BF16)
        middle[b * BLOCK : (b + 1) * BLOCK, :] = jnp.dot(
            trace, whitening[...], preferred_element_type=F32
        ).astype(BF16)
    for c in range(4):
        part = slice(c * 256, (c + 1) * 256)
        place[part, 0:HEAD] = rows[part, 0:HEAD].astype(BF16)
        place[part, HEAD:EDGE] = rows[part, LATE:PLACE].astype(BF16)
        found[part, :] = jnp.dot(
            rows[part, HEAD:LATE].astype(BF16), middle[0 : LATE - HEAD, :],
            preferred_element_type=F32,
        )


def inner(raw, taps, whitening, basis, times):
    return call(
        inner_kernel,
        (
            jax.ShapeDtypeStruct((SPK * 8, CH), F32),
            jax.ShapeDtypeStruct((MIDDLE, CH), BF16),
            jax.ShapeDtypeStruct((SPK * 8, EDGE), BF16),
            jax.ShapeDtypeStruct((2 * BLOCK, SPAN), BF16),
        ),
        [VMEM, VMEM, VMEM, VMEM, SMEM],
        (VMEM, VMEM, VMEM, VMEM),
        [
            pltpu.VMEM((8, SPAN), F32),
            pltpu.VMEM((8, 256), F32),
            pltpu.VMEM((SPK * 8, PLACE), F32),
        ],
        flops=2_000_000_000,
        moved=6_000_000,
    )(raw, taps, whitening, basis, times)


def features_kernel(
    before, after, raw, whitening, found, middle, place, band, project, out,
    window, white, comps, flat,
):
    window[0:BEFORE, :] = before[...]
    window[BEFORE:SPAN, :] = raw[0 : SPAN - BEFORE, :]
    window[SPAN : 2 * SPAN - AFTER, :] = raw[SEG - SPAN + AFTER : SEG, :]
    window[2 * SPAN - AFTER : 2 * SPAN, :] = after[...]
    for b in range(2):
        both = jnp.dot(band[...], window[b * SPAN : (b + 1) * SPAN, :], preferred_element_type=F32)
        trace = (both[0:BLOCK] + both[BLOCK : 2 * BLOCK]).astype(BF16)
        fresh = jnp.dot(trace, whitening[...], preferred_element_type=F32).astype(BF16)
        if b == 0:
            white[0:HEAD, :] = fresh[0:HEAD]
        else:
            white[HEAD + 64 : HEAD + 128, :] = fresh[BLOCK - 64 : BLOCK]
    white[HEAD : HEAD + 64, :] = middle[LATE - HEAD : MIDDLE, :]
    white[HEAD + 128 : EDGE, :] = jnp.zeros((EDGE - HEAD - 128, CH), BF16)
    last = (lax.axis_index("section") == SECTIONS - 1) & (lax.axis_index("lane") == LANES - 1)

    @pl.when(last)
    def _():
        white[HEAD + 64 : HEAD + 128, :] = jnp.zeros((64, CH), BF16)

    for c in range(4):
        part = slice(c * 256, (c + 1) * 256)
        whole = found[part, :] + jnp.dot(place[part, :], white[...], preferred_element_type=F32)
        for i in range(CH // 128):
            comps[i, part, :] = whole[:, i * 128 : (i + 1) * 128]
    for r in range(RANKS):
        for i in range(CH // 128):
            flat[:, r * CH + i * 128 : r * CH + (i + 1) * 128] = comps[
                i, pl.ds(r, SPK, stride=8), :
            ].astype(BF16)
    out[...] = jnp.dot(flat[...], project[...], preferred_element_type=F32).astype(BF16)


def features(before, after, raw, whitening, found, middle, place, band, project):
    return call(
        features_kernel,
        jax.ShapeDtypeStruct((SPK, FEAT), BF16),
        [VMEM] * 9,
        VMEM,
        [
            pltpu.VMEM((2 * SPAN, CH), BF16),
            pltpu.VMEM((EDGE, CH), BF16),
            pltpu.VMEM((CH // 128, SPK * 8, 128), F32),
            pltpu.VMEM((SPK, RANKS * CH), BF16),
        ],
        flops=1_000_000_000,
        moved=6_000_000,
    )(before, after, raw, whitening, found, middle, place, band, project)


def scores_kernel(spikes, centers, counts, shares, weights, tops, logits):
    for b in range(4):
        block = spikes[b * 256 : (b + 1) * 256, :]
        top = None
        for k in range(4):
            part = lax.dot_general(
                centers[0, k * 256 : (k + 1) * 256, :],
                block,
                (((1,), (1,)), ((), ())),
                preferred_element_type=F32,
            ) * (SHARPNESS * LOG2E)
            logits[k * 256 : (k + 1) * 256, b * 256 : (b + 1) * 256] = part
            best = jnp.max(part, axis=0, keepdims=True)
            top = best if top is None else jnp.maximum(top, best)
        total = jnp.zeros((1, 256), F32)
        for k in range(4):
            part = jnp.exp2(logits[k * 256 : (k + 1) * 256, b * 256 : (b + 1) * 256] - top)
            total = total + jnp.sum(part, axis=0, keepdims=True)
            weights[k * 256 : (k + 1) * 256, b * 256 : (b + 1) * 256] = part.astype(BF16)
        lse = top + jnp.log2(total)
        for h in range(2):
            g = 2 * b + h
            mine = lse[:, h * 128 : (h + 1) * 128]
            slot = lax.broadcasted_iota(jnp.int32, (1, 128), 1)
            dead = (lax.axis_index("group") == g) & (slot >= counts[0, 0])
            tops[g : g + 1, :] = top[:, h * 128 : (h + 1) * 128]
            shares[:, g, :] = jnp.broadcast_to(jnp.where(dead, DEAD, mine), (GROUP, 128))


def scores(spikes, centers, counts):
    return call(
        scores_kernel,
        (
            jax.ShapeDtypeStruct((GROUP, GROUP, SPK), F32),
            jax.ShapeDtypeStruct((CG, GROUP * SPK), BF16),
            jax.ShapeDtypeStruct((GROUP, SPK), F32),
        ),
        [VMEM, VMEM, SMEM],
        (VMEM, VMEM, VMEM),
        [pltpu.VMEM((CG, GROUP * SPK), F32)],
        flops=1_000_000_000,
        moved=4_000_000,
    )(spikes, centers, counts)


def sums_kernel(shares, weights, tops, spikes, out):
    best = shares[0]
    for g in range(1, GROUP):
        best = jnp.maximum(best, shares[g])
    total = jnp.zeros_like(best)
    for g in range(GROUP):
        total = total + jnp.exp2(shares[g] - best)
    scale = jnp.exp2(tops[...] - best) / total
    ones = jnp.ones((256, 128), BF16)
    row = lax.broadcasted_iota(jnp.int32, (ROWS, 128), 0)
    lane = lax.broadcasted_iota(jnp.int32, (ROWS, 128), 1)
    pick = row == (lane & (ROWS - 1))
    front = lax.broadcasted_iota(jnp.int32, (1, 128), 1) < ROWS
    masses = [[] for _ in range(NEAR)]
    for k in range(4):
        acc = None
        for b in range(4):
            parts = []
            for h in range(2):
                g = 2 * b + h
                wide = weights[k * 256 : (k + 1) * 256, g * 128 : (g + 1) * 128].astype(F32)
                parts.append((wide * scale[g : g + 1, :]).astype(BF16))
            resp = jnp.concatenate(parts, axis=1)
            rhs = jnp.concatenate([spikes[b * 256 : (b + 1) * 256, :], ones], axis=1)
            term = jnp.dot(resp, rhs, preferred_element_type=F32)
            acc = term if acc is None else acc + term
        for i in range(4):
            owner = 4 * k + i
            far, near = owner // NEAR, owner % NEAR
            rows = acc[i * ROWS : (i + 1) * ROWS, :]
            for c in range(3):
                start = far * SUM_ROWS + c * ROWS
                out[near, start : start + ROWS, :] = rows[:, c * 128 : (c + 1) * 128].astype(BF16)
            mass = jnp.sum(jnp.where(pick, rows[:, 384:512], 0.0), axis=0, keepdims=True)
            masses[near].append(mass)
    slot = lax.broadcasted_iota(jnp.int32, (16, 128), 0)
    for near in range(NEAR):
        block = jnp.zeros((16, 128), F32)
        for far in range(FAR):
            block = jnp.where(slot == far, jnp.broadcast_to(masses[near][far], (16, 128)), block)
        high = block.astype(BF16).astype(F32)
        out[near, FAR * SUM_ROWS : NEAR_ROWS, :] = jnp.where(front, high, block - high).astype(BF16)


def split(mass, front):
    high = mass.astype(BF16).astype(F32)
    return jnp.broadcast_to(
        jnp.where(front, high, mass - high), (PAY - SUM_ROWS, 128)
    ).astype(BF16)


def sums(shares, weights, tops, spikes):
    return call(
        sums_kernel,
        jax.ShapeDtypeStruct((NEAR, NEAR_ROWS, 128), BF16),
        [VMEM] * 4,
        VMEM,
        flops=1_000_000_000,
        moved=4_000_000,
    )(shares, weights, tops, spikes)


def near_kernel(got, own, one, two, three):
    front = lax.broadcasted_iota(jnp.int32, (1, 128), 1) < ROWS
    slot = lax.broadcasted_iota(jnp.int32, (16, 128), 0)
    mine = lax.axis_index("lane") // NEAR
    tails = got[0, FAR * SUM_ROWS : NEAR_ROWS, :].astype(F32)
    for n in range(1, NEAR):
        tails = tails + got[n, FAR * SUM_ROWS : NEAR_ROWS, :].astype(F32)
    for d, out in enumerate((own, one, two, three)):
        far = lax.rem(mine + d, FAR)
        part = pl.ds(pl.multiple_of(far * SUM_ROWS, 64), SUM_ROWS)
        acc = got[0, part, :].astype(F32)
        for n in range(1, NEAR):
            acc = acc + got[n, part, :].astype(F32)
        tail = jnp.sum(jnp.where(slot == far, tails, 0.0), axis=0, keepdims=True)
        mass = tail + pltpu.roll(tail, ROWS, 1)
        out[0:SUM_ROWS, :] = acc.astype(out.dtype)
        if d == 0:
            out[SUM_ROWS:PAY, :] = jnp.broadcast_to(mass, (PAY - SUM_ROWS, 128))
        else:
            out[SUM_ROWS:PAY, :] = split(mass, front)


def far_kernel(own, one, two, three, out, sent):
    front = lax.broadcasted_iota(jnp.int32, (1, 128), 1) < ROWS
    acc = one[...].astype(F32) + two[...].astype(F32) + three[...].astype(F32)
    total = own[0:SUM_ROWS, :] + acc[0:SUM_ROWS]
    tail = acc[SUM_ROWS:PAY, :]
    mass = own[SUM_ROWS:PAY, :] + tail + pltpu.roll(tail, ROWS, 1)
    out[0:SUM_ROWS, :] = total
    out[SUM_ROWS:PAY, :] = mass
    sent[0:SUM_ROWS, :] = total.astype(BF16)
    sent[SUM_ROWS:PAY, :] = split(mass[0:1], front)


def final_kernel(own, one, two, three, centers, prior, out, held, sem):
    lane_at = lax.axis_index("lane")
    copy = pltpu.make_async_copy(
        centers.at[0, pl.ds(pl.multiple_of(lane_at * ROWS, ROWS), ROWS)], held, sem
    )
    copy.start()
    past = one[...].astype(F32) + two[...].astype(F32) + three[...].astype(F32)
    acc = own[0:SUM_ROWS, :] + past[0:SUM_ROWS]
    tail = past[SUM_ROWS : SUM_ROWS + 1, :]
    mass = own[SUM_ROWS : SUM_ROWS + 1, :] + tail + pltpu.roll(tail, ROWS, 1)
    row = lax.broadcasted_iota(jnp.int32, (ROWS, ROWS), 0)
    lane = lax.broadcasted_iota(jnp.int32, (ROWS, ROWS), 1)
    pick = row == lane

    def column(value):
        wide = jnp.broadcast_to(value, (ROWS, ROWS))
        return jnp.sum(jnp.where(pick, wide, 0.0), axis=1, keepdims=True)

    weight = column(prior[...])
    inverse = 1.0 / (weight + column(mass[:, 0:ROWS]))
    copy.wait()
    for c in range(3):
        numer = weight * held[:, c * 128 : (c + 1) * 128].astype(F32) + acc[
            c * ROWS : (c + 1) * ROWS, :
        ]
        out[0, 0, :, c * 128 : (c + 1) * 128] = numer * inverse


def per_device(raw, taps, whitening, basis, project, centroids, prior, times, counts):
    windows = ("section", "lane")
    count = SECTIONS * LANES
    head, tail = call(
        edges_kernel,
        (jax.ShapeDtypeStruct((AFTER, CH), BF16), jax.ShapeDtypeStruct((BEFORE, CH), BF16)),
        [VMEM],
        (VMEM, VMEM),
        moved=1_000_000,
    )(raw)
    before = lax.ppermute(tail, windows, [(i, i + 1) for i in range(count - 1)])
    after = lax.ppermute(head, windows, [(i + 1, i) for i in range(count - 1)])
    held = inner(raw, taps.reshape(1, TAPS), whitening, basis.T, times)
    feats = features(before, after, raw, whitening, *held, project)
    spikes = lax.all_gather(feats, "group", axis=0, tiled=True)
    shares, weights, tops = scores(spikes, centroids, counts)
    shares = lax.all_to_all(shares, "group", 0, 0)
    parts = sums(shares, weights, tops, spikes)
    near = [[NEAR * far + n for n in range(NEAR)] for far in range(FAR)]
    got = lax.all_to_all(parts, "lane", 0, 0, axis_index_groups=near)
    small = jax.ShapeDtypeStruct((PAY, 128), BF16)
    wide = jax.ShapeDtypeStruct((PAY, 128), F32)
    own, *sent = call(
        near_kernel, (wide, small, small, small), [VMEM], (VMEM,) * 4, moved=1_000_000
    )(got)
    took = [
        lax.ppermute(part, "lane", [(i, (i + NEAR * (d + 1)) % LANES) for i in range(LANES)])
        for d, part in enumerate(sent)
    ]
    total, sent = call(far_kernel, (wide, small), [VMEM] * 4, (VMEM,) * 2, moved=300_000)(own, *took)
    earlier = [
        lax.ppermute(sent, "section", [(i, i + d) for i in range(SECTIONS - d)])
        for d in range(1, SECTIONS)
    ]
    return call(
        final_kernel,
        jax.ShapeDtypeStruct((1, 1, ROWS, FEAT), F32),
        [VMEM, VMEM, VMEM, VMEM, ANY, VMEM],
        VMEM,
        [pltpu.VMEM((ROWS, FEAT), BF16), pltpu.SemaphoreType.DMA],
        moved=600_000,
    )(total, *earlier, centroids, prior)


def solution(mesh):
    placed = (
        P(("section", "lane"), "group"),
        P(),
        P("group", None),
        P(),
        P(),
        P("group", None, None),
        P("group", "lane"),
        P(("section", "lane"), "group", None),
        P(("section", "lane"), "group"),
    )
    return jax.shard_map(
        per_device,
        mesh=mesh,
        in_specs=placed,
        out_specs=P("section", "group", "lane", None),
        check_vma=False,
    )
```

```python
import functools
import math

import jax
import jax.numpy as jnp
from jax import lax
from jax.experimental import pallas as pl
from jax.experimental.pallas import tpu as pltpu
from jax.sharding import PartitionSpec as P

F32 = jnp.float32
BF16 = jnp.bfloat16
LOG2E = math.log2(math.e)
SHARPNESS = 0.25
DEAD = 1e30

SEG = 1024
CH = 384
FEAT = 384
SPK = 128
TAPS = 64
SNIP = 121
HALF = 60
RANKS = 6
GROUP = 8
LANES = 16
SECTIONS = 4
NEAR = 4
FAR = 4
CG = 1024
ROWS = 64
BEFORE = 128
AFTER = 64
BLOCK = 192
SPAN = BLOCK + TAPS
PLACE = 1280
HEAD = 128
LATE = 1024
MIDDLE = 960
EDGE = HEAD + PLACE - LATE
PAY = 208
SUM_ROWS = 192
NEAR_ROWS = FAR * SUM_ROWS + 16
VMEM_LIMIT = 20 * 1024 * 1024

VMEM = pl.BlockSpec(memory_space=pltpu.VMEM)
SMEM = pl.BlockSpec(memory_space=pltpu.SMEM)
ANY = pl.BlockSpec(memory_space=pl.ANY)


def call(kernel, out_shape, in_specs, out_specs, scratch=(), flops=0, moved=0):
    return pl.pallas_call(
        kernel,
        out_shape=out_shape,
        in_specs=in_specs,
        out_specs=out_specs,
        scratch_shapes=list(scratch),
        compiler_params=pltpu.CompilerParams(vmem_limit_bytes=VMEM_LIMIT),
        cost_estimate=pl.CostEstimate(flops=flops, bytes_accessed=moved, transcendentals=0),
    )


def edges_kernel(raw, head, tail):
    head[...] = raw[0:AFTER, :]
    tail[...] = raw[SEG - BEFORE : SEG, :]


def place_kernel(taps, basis, times, core, place, band, row, snip, rows):
    row[...] = jnp.zeros_like(row)
    row[0:1, 0:TAPS] = taps[...]
    spread = jnp.broadcast_to(row[0:1, :], (SPAN, SPAN))
    shifted = pltpu.roll(spread, SPAN - TAPS, 1, stride=1, stride_axis=0)
    table = jnp.transpose(shifted)[0:BLOCK, :]
    high = table.astype(BF16)
    band[0:BLOCK, :] = high
    band[BLOCK : 2 * BLOCK, :] = (table - high.astype(F32)).astype(BF16)

    snip[...] = jnp.zeros_like(snip)
    snip[0:RANKS, 0:SNIP] = basis[...].astype(F32)
    shape = snip[...]
    rows[...] = jnp.zeros_like(rows)

    def put(s, carry):
        u = times[0, 0, s] + (64 - HALF)
        start = pl.multiple_of((u >> 7) * 128, 128)
        at = pl.multiple_of(s * 8, 8)
        rows[pl.ds(at, 8), pl.ds(start, 256)] = pltpu.roll(shape, u & 127, 1)
        return carry

    lax.fori_loop(0, SPK, put, 0, unroll=128)

    place[:, 0:HEAD] = rows[:, 0:HEAD].astype(BF16)
    place[:, HEAD:EDGE] = rows[:, LATE:PLACE].astype(BF16)
    core[...] = rows[:, HEAD:LATE].astype(BF16)


def inner_kernel(raw, whitening, core, band, found, middle):
    for b in range(5):
        both = jnp.dot(
            band[...], raw[b * BLOCK : b * BLOCK + SPAN, :], preferred_element_type=F32
        )
        trace = (both[0:BLOCK] + both[BLOCK : 2 * BLOCK]).astype(BF16)
        middle[b * BLOCK : (b + 1) * BLOCK, :] = jnp.dot(
            trace, whitening[...], preferred_element_type=F32
        ).astype(BF16)
    for c in range(4):
        part = slice(c * 256, (c + 1) * 256)
        found[part, :] = jnp.dot(
            core[part, :], middle[0 : LATE - HEAD, :], preferred_element_type=F32
        )


def inner(raw, taps, whitening, basis, times):
    core, place, band = call(
        place_kernel,
        (
            jax.ShapeDtypeStruct((SPK * 8, LATE - HEAD), BF16),
            jax.ShapeDtypeStruct((SPK * 8, EDGE), BF16),
            jax.ShapeDtypeStruct((2 * BLOCK, SPAN), BF16),
        ),
        [VMEM, VMEM, SMEM],
        (VMEM, VMEM, VMEM),
        [
            pltpu.VMEM((8, SPAN), F32),
            pltpu.VMEM((8, 256), F32),
            pltpu.VMEM((SPK * 8, PLACE), F32),
        ],
        flops=500_000_000,
        moved=8_000_000,
    )(taps, basis, times)
    found, middle = call(
        inner_kernel,
        (
            jax.ShapeDtypeStruct((SPK * 8, CH), F32),
            jax.ShapeDtypeStruct((MIDDLE, CH), BF16),
        ),
        [VMEM] * 4,
        (VMEM, VMEM),
        flops=2_000_000_000,
        moved=6_000_000,
    )(raw, whitening, core, band)
    return found, middle, place, band


def features_kernel(
    before, after, raw, whitening, found, middle, place, band, project, out,
    window, white, comps, flat,
):
    window[0:BEFORE, :] = before[...]
    window[BEFORE:SPAN, :] = raw[0 : SPAN - BEFORE, :]
    window[SPAN : 2 * SPAN - AFTER, :] = raw[SEG - SPAN + AFTER : SEG, :]
    window[2 * SPAN - AFTER : 2 * SPAN, :] = after[...]
    for b in range(2):
        both = jnp.dot(band[...], window[b * SPAN : (b + 1) * SPAN, :], preferred_element_type=F32)
        trace = (both[0:BLOCK] + both[BLOCK : 2 * BLOCK]).astype(BF16)
        fresh = jnp.dot(trace, whitening[...], preferred_element_type=F32).astype(BF16)
        if b == 0:
            white[0:HEAD, :] = fresh[0:HEAD]
        else:
            white[HEAD + 64 : HEAD + 128, :] = fresh[BLOCK - 64 : BLOCK]
    white[HEAD : HEAD + 64, :] = middle[LATE - HEAD : MIDDLE, :]
    white[HEAD + 128 : EDGE, :] = jnp.zeros((EDGE - HEAD - 128, CH), BF16)
    last = (lax.axis_index("section") == SECTIONS - 1) & (lax.axis_index("lane") == LANES - 1)

    @pl.when(last)
    def _():
        white[HEAD + 64 : HEAD + 128, :] = jnp.zeros((64, CH), BF16)

    for c in range(4):
        part = slice(c * 256, (c + 1) * 256)
        whole = found[part, :] + jnp.dot(place[part, :], white[...], preferred_element_type=F32)
        for i in range(CH // 128):
            comps[i, part, :] = whole[:, i * 128 : (i + 1) * 128]
    for r in range(RANKS):
        for i in range(CH // 128):
            flat[:, r * CH + i * 128 : r * CH + (i + 1) * 128] = comps[
                i, pl.ds(r, SPK, stride=8), :
            ].astype(BF16)
    out[...] = jnp.dot(flat[...], project[...], preferred_element_type=F32).astype(BF16)


def features(before, after, raw, whitening, found, middle, place, band, project):
    return call(
        features_kernel,
        jax.ShapeDtypeStruct((SPK, FEAT), BF16),
        [VMEM] * 9,
        VMEM,
        [
            pltpu.VMEM((2 * SPAN, CH), BF16),
            pltpu.VMEM((EDGE, CH), BF16),
            pltpu.VMEM((CH // 128, SPK * 8, 128), F32),
            pltpu.VMEM((SPK, RANKS * CH), BF16),
        ],
        flops=1_000_000_000,
        moved=6_000_000,
    )(before, after, raw, whitening, found, middle, place, band, project)


def scores_kernel(spikes, centers, counts, shares, weights, tops, logits):
    for b in range(4):
        block = spikes[b * 256 : (b + 1) * 256, :]
        top = None
        for k in range(4):
            part = lax.dot_general(
                centers[0, k * 256 : (k + 1) * 256, :],
                block,
                (((1,), (1,)), ((), ())),
                preferred_element_type=F32,
            ) * (SHARPNESS * LOG2E)
            logits[k * 256 : (k + 1) * 256, b * 256 : (b + 1) * 256] = part
            best = jnp.max(part, axis=0, keepdims=True)
            top = best if top is None else jnp.maximum(top, best)
        total = jnp.zeros((1, 256), F32)
        for k in range(4):
            part = jnp.exp2(logits[k * 256 : (k + 1) * 256, b * 256 : (b + 1) * 256] - top)
            total = total + jnp.sum(part, axis=0, keepdims=True)
            weights[k * 256 : (k + 1) * 256, b * 256 : (b + 1) * 256] = part.astype(BF16)
        lse = top + jnp.log2(total)
        for h in range(2):
            g = 2 * b + h
            mine = lse[:, h * 128 : (h + 1) * 128]
            slot = lax.broadcasted_iota(jnp.int32, (1, 128), 1)
            dead = (lax.axis_index("group") == g) & (slot >= counts[0, 0])
            tops[g : g + 1, :] = top[:, h * 128 : (h + 1) * 128]
            shares[:, g, :] = jnp.broadcast_to(jnp.where(dead, DEAD, mine), (GROUP, 128))


def scores(spikes, centers, counts):
    return call(
        scores_kernel,
        (
            jax.ShapeDtypeStruct((GROUP, GROUP, SPK), F32),
            jax.ShapeDtypeStruct((CG, GROUP * SPK), BF16),
            jax.ShapeDtypeStruct((GROUP, SPK), F32),
        ),
        [VMEM, VMEM, SMEM],
        (VMEM, VMEM, VMEM),
        [pltpu.VMEM((CG, GROUP * SPK), F32)],
        flops=1_000_000_000,
        moved=4_000_000,
    )(spikes, centers, counts)


def sums_kernel(shares, weights, tops, spikes, out):
    best = shares[0]
    for g in range(1, GROUP):
        best = jnp.maximum(best, shares[g])
    total = jnp.zeros_like(best)
    for g in range(GROUP):
        total = total + jnp.exp2(shares[g] - best)
    scale = jnp.exp2(tops[...] - best) / total
    ones = jnp.ones((256, 128), BF16)
    row = lax.broadcasted_iota(jnp.int32, (ROWS, 128), 0)
    lane = lax.broadcasted_iota(jnp.int32, (ROWS, 128), 1)
    pick = row == (lane & (ROWS - 1))
    front = lax.broadcasted_iota(jnp.int32, (1, 128), 1) < ROWS
    masses = [[] for _ in range(NEAR)]
    for k in range(4):
        acc = None
        for b in range(4):
            parts = []
            for h in range(2):
                g = 2 * b + h
                wide = weights[k * 256 : (k + 1) * 256, g * 128 : (g + 1) * 128].astype(F32)
                parts.append((wide * scale[g : g + 1, :]).astype(BF16))
            resp = jnp.concatenate(parts, axis=1)
            rhs = jnp.concatenate([spikes[b * 256 : (b + 1) * 256, :], ones], axis=1)
            term = jnp.dot(resp, rhs, preferred_element_type=F32)
            acc = term if acc is None else acc + term
        for i in range(4):
            owner = 4 * k + i
            far, near = owner // NEAR, owner % NEAR
            rows = acc[i * ROWS : (i + 1) * ROWS, :]
            for c in range(3):
                start = far * SUM_ROWS + c * ROWS
                out[near, start : start + ROWS, :] = rows[:, c * 128 : (c + 1) * 128].astype(BF16)
            mass = jnp.sum(jnp.where(pick, rows[:, 384:512], 0.0), axis=0, keepdims=True)
            masses[near].append(mass)
    slot = lax.broadcasted_iota(jnp.int32, (16, 128), 0)
    for near in range(NEAR):
        block = jnp.zeros((16, 128), F32)
        for far in range(FAR):
            block = jnp.where(slot == far, jnp.broadcast_to(masses[near][far], (16, 128)), block)
        high = block.astype(BF16).astype(F32)
        out[near, FAR * SUM_ROWS : NEAR_ROWS, :] = jnp.where(front, high, block - high).astype(BF16)


def split(mass, front):
    high = mass.astype(BF16).astype(F32)
    return jnp.broadcast_to(
        jnp.where(front, high, mass - high), (PAY - SUM_ROWS, 128)
    ).astype(BF16)


def sums(shares, weights, tops, spikes):
    return call(
        sums_kernel,
        jax.ShapeDtypeStruct((NEAR, NEAR_ROWS, 128), BF16),
        [VMEM] * 4,
        VMEM,
        flops=1_000_000_000,
        moved=4_000_000,
    )(shares, weights, tops, spikes)


def near_kernel(got, own, one, two, three):
    front = lax.broadcasted_iota(jnp.int32, (1, 128), 1) < ROWS
    slot = lax.broadcasted_iota(jnp.int32, (16, 128), 0)
    mine = lax.axis_index("lane") // NEAR
    tails = got[0, FAR * SUM_ROWS : NEAR_ROWS, :].astype(F32)
    for n in range(1, NEAR):
        tails = tails + got[n, FAR * SUM_ROWS : NEAR_ROWS, :].astype(F32)
    for d, out in enumerate((own, one, two, three)):
        far = lax.rem(mine + d, FAR)
        part = pl.ds(pl.multiple_of(far * SUM_ROWS, 64), SUM_ROWS)
        acc = got[0, part, :].astype(F32)
        for n in range(1, NEAR):
            acc = acc + got[n, part, :].astype(F32)
        tail = jnp.sum(jnp.where(slot == far, tails, 0.0), axis=0, keepdims=True)
        mass = tail + pltpu.roll(tail, ROWS, 1)
        out[0:SUM_ROWS, :] = acc.astype(out.dtype)
        if d == 0:
            out[SUM_ROWS:PAY, :] = jnp.broadcast_to(mass, (PAY - SUM_ROWS, 128))
        else:
            out[SUM_ROWS:PAY, :] = split(mass, front)


def far_kernel(own, one, two, three, out, sent):
    front = lax.broadcasted_iota(jnp.int32, (1, 128), 1) < ROWS
    acc = one[...].astype(F32) + two[...].astype(F32) + three[...].astype(F32)
    total = own[0:SUM_ROWS, :] + acc[0:SUM_ROWS]
    tail = acc[SUM_ROWS:PAY, :]
    mass = own[SUM_ROWS:PAY, :] + tail + pltpu.roll(tail, ROWS, 1)
    out[0:SUM_ROWS, :] = total
    out[SUM_ROWS:PAY, :] = mass
    sent[0:SUM_ROWS, :] = total.astype(BF16)
    sent[SUM_ROWS:PAY, :] = split(mass[0:1], front)


def final_kernel(own, one, two, three, centers, prior, out, held, sem):
    lane_at = lax.axis_index("lane")
    copy = pltpu.make_async_copy(
        centers.at[0, pl.ds(pl.multiple_of(lane_at * ROWS, ROWS), ROWS)], held, sem
    )
    copy.start()
    past = one[...].astype(F32) + two[...].astype(F32) + three[...].astype(F32)
    acc = own[0:SUM_ROWS, :] + past[0:SUM_ROWS]
    tail = past[SUM_ROWS : SUM_ROWS + 1, :]
    mass = own[SUM_ROWS : SUM_ROWS + 1, :] + tail + pltpu.roll(tail, ROWS, 1)
    row = lax.broadcasted_iota(jnp.int32, (ROWS, ROWS), 0)
    lane = lax.broadcasted_iota(jnp.int32, (ROWS, ROWS), 1)
    pick = row == lane

    def column(value):
        wide = jnp.broadcast_to(value, (ROWS, ROWS))
        return jnp.sum(jnp.where(pick, wide, 0.0), axis=1, keepdims=True)

    weight = column(prior[...])
    inverse = 1.0 / (weight + column(mass[:, 0:ROWS]))
    copy.wait()
    for c in range(3):
        numer = weight * held[:, c * 128 : (c + 1) * 128].astype(F32) + acc[
            c * ROWS : (c + 1) * ROWS, :
        ]
        out[0, 0, :, c * 128 : (c + 1) * 128] = numer * inverse


def per_device(raw, taps, whitening, basis, project, centroids, prior, times, counts):
    windows = ("section", "lane")
    count = SECTIONS * LANES
    head, tail = call(
        edges_kernel,
        (jax.ShapeDtypeStruct((AFTER, CH), BF16), jax.ShapeDtypeStruct((BEFORE, CH), BF16)),
        [VMEM],
        (VMEM, VMEM),
        moved=1_000_000,
    )(raw)
    before = lax.ppermute(tail, windows, [(i, i + 1) for i in range(count - 1)])
    after = lax.ppermute(head, windows, [(i + 1, i) for i in range(count - 1)])
    held = inner(raw, taps.reshape(1, TAPS), whitening, basis.T, times)
    feats = features(before, after, raw, whitening, *held, project)
    spikes = lax.all_gather(feats, "group", axis=0, tiled=True)
    shares, weights, tops = scores(spikes, centroids, counts)
    shares = lax.all_to_all(shares, "group", 0, 0)
    parts = sums(shares, weights, tops, spikes)
    near = [[NEAR * far + n for n in range(NEAR)] for far in range(FAR)]
    got = lax.all_to_all(parts, "lane", 0, 0, axis_index_groups=near)
    small = jax.ShapeDtypeStruct((PAY, 128), BF16)
    wide = jax.ShapeDtypeStruct((PAY, 128), F32)
    own, *sent = call(
        near_kernel, (wide, small, small, small), [VMEM], (VMEM,) * 4, moved=1_000_000
    )(got)
    took = [
        lax.ppermute(part, "lane", [(i, (i + NEAR * (d + 1)) % LANES) for i in range(LANES)])
        for d, part in enumerate(sent)
    ]
    total, sent = call(far_kernel, (wide, small), [VMEM] * 4, (VMEM,) * 2, moved=300_000)(own, *took)
    earlier = [
        lax.ppermute(sent, "section", [(i, i + d) for i in range(SECTIONS - d)])
        for d in range(1, SECTIONS)
    ]
    return call(
        final_kernel,
        jax.ShapeDtypeStruct((1, 1, ROWS, FEAT), F32),
        [VMEM, VMEM, VMEM, VMEM, ANY, VMEM],
        VMEM,
        [pltpu.VMEM((ROWS, FEAT), BF16), pltpu.SemaphoreType.DMA],
        moved=600_000,
    )(total, *earlier, centroids, prior)


def solution(mesh):
    placed = (
        P(("section", "lane"), "group"),
        P(),
        P("group", None),
        P(),
        P(),
        P("group", None, None),
        P("group", "lane"),
        P(("section", "lane"), "group", None),
        P(("section", "lane"), "group"),
    )
    return jax.shard_map(
        per_device,
        mesh=mesh,
        in_specs=placed,
        out_specs=P("section", "group", "lane", None),
        check_vma=False,
    )
```

```python
import functools
import math

import jax
import jax.numpy as jnp
from jax import lax
from jax.experimental import pallas as pl
from jax.experimental.pallas import tpu as pltpu
from jax.sharding import PartitionSpec as P

F32 = jnp.float32
BF16 = jnp.bfloat16
LOG2E = math.log2(math.e)
SHARPNESS = 0.25
DEAD = 1e30

SEG = 1024
CH = 384
FEAT = 384
SPK = 128
TAPS = 64
SNIP = 121
HALF = 60
RANKS = 6
GROUP = 8
LANES = 16
SECTIONS = 4
NEAR = 4
FAR = 4
CG = 1024
ROWS = 64
BEFORE = 128
AFTER = 64
BLOCK = 192
SPAN = BLOCK + TAPS
PLACE = 1280
HEAD = 128
LATE = 1024
MIDDLE = 960
EDGE = HEAD + PLACE - LATE
PAY = 208
SUM_ROWS = 192
NEAR_ROWS = FAR * SUM_ROWS + 16
VMEM_LIMIT = 20 * 1024 * 1024

VMEM = pl.BlockSpec(memory_space=pltpu.VMEM)
SMEM = pl.BlockSpec(memory_space=pltpu.SMEM)
ANY = pl.BlockSpec(memory_space=pl.ANY)


def call(kernel, out_shape, in_specs, out_specs, scratch=(), flops=0, moved=0):
    return pl.pallas_call(
        kernel,
        out_shape=out_shape,
        in_specs=in_specs,
        out_specs=out_specs,
        scratch_shapes=list(scratch),
        compiler_params=pltpu.CompilerParams(vmem_limit_bytes=VMEM_LIMIT),
        cost_estimate=pl.CostEstimate(flops=flops, bytes_accessed=moved, transcendentals=0),
    )


def edges_kernel(raw, head, tail):
    head[...] = raw[0:AFTER, :]
    tail[...] = raw[SEG - BEFORE : SEG, :]


def place_kernel(taps, basis, times, core, place, band, row, snip, rows):
    row[...] = jnp.zeros_like(row)
    row[0:1, 0:TAPS] = taps[...]
    spread = jnp.broadcast_to(row[0:1, :], (SPAN, SPAN))
    shifted = pltpu.roll(spread, SPAN - TAPS, 1, stride=1, stride_axis=0)
    table = jnp.transpose(shifted)[0:BLOCK, :]
    high = table.astype(BF16)
    band[0:BLOCK, :] = high
    band[BLOCK : 2 * BLOCK, :] = (table - high.astype(F32)).astype(BF16)

    snip[...] = jnp.zeros_like(snip)
    snip[0:RANKS, 0:SNIP] = basis[...].astype(F32)
    shape = snip[...]
    rows[...] = jnp.zeros_like(rows)

    def put(s, carry):
        u = times[0, 0, s] + (64 - HALF)
        start = pl.multiple_of((u >> 7) * 128, 128)
        at = pl.multiple_of(s * 8, 8)
        rows[pl.ds(at, 8), pl.ds(start, 256)] = pltpu.roll(shape, u & 127, 1)
        return carry

    lax.fori_loop(0, SPK, put, 0, unroll=128)

    place[:, 0:HEAD] = rows[:, 0:HEAD].astype(BF16)
    place[:, HEAD:EDGE] = rows[:, LATE:PLACE].astype(BF16)
    core[...] = rows[:, HEAD:LATE].astype(BF16)


def inner_kernel(raw, whitening, core, band, found, middle):
    for b in range(5):
        both = jnp.dot(
            band[...], raw[b * BLOCK : b * BLOCK + SPAN, :], preferred_element_type=F32
        )
        trace = (both[0:BLOCK] + both[BLOCK : 2 * BLOCK]).astype(BF16)
        middle[b * BLOCK : (b + 1) * BLOCK, :] = jnp.dot(
            trace, whitening[...], preferred_element_type=F32
        ).astype(BF16)
    for c in range(4):
        part = slice(c * 256, (c + 1) * 256)
        found[part, :] = jnp.dot(
            core[part, :], middle[0 : LATE - HEAD, :], preferred_element_type=F32
        )


def inner(raw, taps, whitening, basis, times):
    core, place, band = call(
        place_kernel,
        (
            jax.ShapeDtypeStruct((SPK * 8, LATE - HEAD), BF16),
            jax.ShapeDtypeStruct((SPK * 8, EDGE), BF16),
            jax.ShapeDtypeStruct((2 * BLOCK, SPAN), BF16),
        ),
        [VMEM, VMEM, SMEM],
        (VMEM, VMEM, VMEM),
        [
            pltpu.VMEM((8, SPAN), F32),
            pltpu.VMEM((8, 256), F32),
            pltpu.VMEM((SPK * 8, PLACE), F32),
        ],
        flops=500_000_000,
        moved=8_000_000,
    )(taps, basis, times)
    found, middle = call(
        inner_kernel,
        (
            jax.ShapeDtypeStruct((SPK * 8, CH), F32),
            jax.ShapeDtypeStruct((MIDDLE, CH), BF16),
        ),
        [VMEM] * 4,
        (VMEM, VMEM),
        flops=2_000_000_000,
        moved=6_000_000,
    )(raw, whitening, core, band)
    return found, middle, place, band


def features_kernel(
    before, after, raw, whitening, found, middle, place, band, project, out,
    window, white, comps, flat,
):
    window[0:BEFORE, :] = before[...]
    window[BEFORE:SPAN, :] = raw[0 : SPAN - BEFORE, :]
    window[SPAN : 2 * SPAN - AFTER, :] = raw[SEG - SPAN + AFTER : SEG, :]
    window[2 * SPAN - AFTER : 2 * SPAN, :] = after[...]
    for b in range(2):
        both = jnp.dot(band[...], window[b * SPAN : (b + 1) * SPAN, :], preferred_element_type=F32)
        trace = (both[0:BLOCK] + both[BLOCK : 2 * BLOCK]).astype(BF16)
        fresh = jnp.dot(trace, whitening[...], preferred_element_type=F32).astype(BF16)
        if b == 0:
            white[0:HEAD, :] = fresh[0:HEAD]
        else:
            white[HEAD + 64 : HEAD + 128, :] = fresh[BLOCK - 64 : BLOCK]
    white[HEAD : HEAD + 64, :] = middle[LATE - HEAD : MIDDLE, :]
    white[HEAD + 128 : EDGE, :] = jnp.zeros((EDGE - HEAD - 128, CH), BF16)
    last = (lax.axis_index("section") == SECTIONS - 1) & (lax.axis_index("lane") == LANES - 1)

    @pl.when(last)
    def _():
        white[HEAD + 64 : HEAD + 128, :] = jnp.zeros((64, CH), BF16)

    for c in range(4):
        part = slice(c * 256, (c + 1) * 256)
        whole = found[part, :] + jnp.dot(place[part, :], white[...], preferred_element_type=F32)
        for i in range(CH // 128):
            comps[i, part, :] = whole[:, i * 128 : (i + 1) * 128]
    for r in range(RANKS):
        for i in range(CH // 128):
            flat[:, r * CH + i * 128 : r * CH + (i + 1) * 128] = comps[
                i, pl.ds(r, SPK, stride=8), :
            ].astype(BF16)
    out[...] = jnp.dot(flat[...], project[...], preferred_element_type=F32).astype(BF16)


def features(before, after, raw, whitening, found, middle, place, band, project):
    return call(
        features_kernel,
        jax.ShapeDtypeStruct((SPK, FEAT), BF16),
        [VMEM] * 9,
        VMEM,
        [
            pltpu.VMEM((2 * SPAN, CH), BF16),
            pltpu.VMEM((EDGE, CH), BF16),
            pltpu.VMEM((CH // 128, SPK * 8, 128), F32),
            pltpu.VMEM((SPK, RANKS * CH), BF16),
        ],
        flops=1_000_000_000,
        moved=6_000_000,
    )(before, after, raw, whitening, found, middle, place, band, project)


def scores_kernel(spikes, centers, counts, shares, weights, tops, logits):
    for b in range(4):
        block = spikes[b * 256 : (b + 1) * 256, :]
        top = None
        for k in range(4):
            part = lax.dot_general(
                centers[0, k * 256 : (k + 1) * 256, :],
                block,
                (((1,), (1,)), ((), ())),
                preferred_element_type=F32,
            ) * (SHARPNESS * LOG2E)
            logits[k * 256 : (k + 1) * 256, b * 256 : (b + 1) * 256] = part
            best = jnp.max(part, axis=0, keepdims=True)
            top = best if top is None else jnp.maximum(top, best)
        total = jnp.zeros((1, 256), F32)
        for k in range(4):
            part = jnp.exp2(logits[k * 256 : (k + 1) * 256, b * 256 : (b + 1) * 256] - top)
            total = total + jnp.sum(part, axis=0, keepdims=True)
            weights[k * 256 : (k + 1) * 256, b * 256 : (b + 1) * 256] = part.astype(BF16)
        lse = top + jnp.log2(total)
        for h in range(2):
            g = 2 * b + h
            mine = lse[:, h * 128 : (h + 1) * 128]
            slot = lax.broadcasted_iota(jnp.int32, (1, 128), 1)
            dead = (lax.axis_index("group") == g) & (slot >= counts[0, 0])
            tops[g : g + 1, :] = top[:, h * 128 : (h + 1) * 128]
            shares[:, g, :] = jnp.broadcast_to(jnp.where(dead, DEAD, mine), (GROUP, 128))


def scores(spikes, centers, counts):
    return call(
        scores_kernel,
        (
            jax.ShapeDtypeStruct((GROUP, GROUP, SPK), F32),
            jax.ShapeDtypeStruct((CG, GROUP * SPK), BF16),
            jax.ShapeDtypeStruct((GROUP, SPK), F32),
        ),
        [VMEM, VMEM, SMEM],
        (VMEM, VMEM, VMEM),
        [pltpu.VMEM((CG, GROUP * SPK), F32)],
        flops=1_000_000_000,
        moved=4_000_000,
    )(spikes, centers, counts)


def sums_kernel(shares, weights, tops, spikes, out):
    best = shares[0]
    for g in range(1, GROUP):
        best = jnp.maximum(best, shares[g])
    total = jnp.zeros_like(best)
    for g in range(GROUP):
        total = total + jnp.exp2(shares[g] - best)
    scale = jnp.exp2(tops[...] - best) / total
    ones = jnp.ones((256, 128), BF16)
    row = lax.broadcasted_iota(jnp.int32, (ROWS, 128), 0)
    lane = lax.broadcasted_iota(jnp.int32, (ROWS, 128), 1)
    pick = row == (lane & (ROWS - 1))
    front = lax.broadcasted_iota(jnp.int32, (1, 128), 1) < ROWS
    masses = [[] for _ in range(NEAR)]
    for k in range(4):
        acc = None
        for b in range(4):
            parts = []
            for h in range(2):
                g = 2 * b + h
                wide = weights[k * 256 : (k + 1) * 256, g * 128 : (g + 1) * 128].astype(F32)
                parts.append((wide * scale[g : g + 1, :]).astype(BF16))
            resp = jnp.concatenate(parts, axis=1)
            rhs = jnp.concatenate([spikes[b * 256 : (b + 1) * 256, :], ones], axis=1)
            term = jnp.dot(resp, rhs, preferred_element_type=F32)
            acc = term if acc is None else acc + term
        for i in range(4):
            owner = 4 * k + i
            far, near = owner // NEAR, owner % NEAR
            rows = acc[i * ROWS : (i + 1) * ROWS, :]
            for c in range(3):
                start = far * SUM_ROWS + c * ROWS
                out[near, start : start + ROWS, :] = rows[:, c * 128 : (c + 1) * 128].astype(BF16)
            mass = jnp.sum(jnp.where(pick, rows[:, 384:512], 0.0), axis=0, keepdims=True)
            masses[near].append(mass)
    slot = lax.broadcasted_iota(jnp.int32, (16, 128), 0)
    for near in range(NEAR):
        block = jnp.zeros((16, 128), F32)
        for far in range(FAR):
            block = jnp.where(slot == far, jnp.broadcast_to(masses[near][far], (16, 128)), block)
        high = block.astype(BF16).astype(F32)
        out[near, FAR * SUM_ROWS : NEAR_ROWS, :] = jnp.where(front, high, block - high).astype(BF16)


def split(mass, front):
    high = mass.astype(BF16).astype(F32)
    return jnp.broadcast_to(
        jnp.where(front, high, mass - high), (PAY - SUM_ROWS, 128)
    ).astype(BF16)


def sums(shares, weights, tops, spikes):
    return call(
        sums_kernel,
        jax.ShapeDtypeStruct((NEAR, NEAR_ROWS, 128), BF16),
        [VMEM] * 4,
        VMEM,
        flops=1_000_000_000,
        moved=4_000_000,
    )(shares, weights, tops, spikes)


def near_kernel(got, out):
    front = lax.broadcasted_iota(jnp.int32, (1, 128), 1) < ROWS
    slot = lax.broadcasted_iota(jnp.int32, (16, 128), 0)
    tails = got[0, FAR * SUM_ROWS : NEAR_ROWS, :].astype(F32)
    for n in range(1, NEAR):
        tails = tails + got[n, FAR * SUM_ROWS : NEAR_ROWS, :].astype(F32)
    for far in range(FAR):
        part = slice(far * SUM_ROWS, (far + 1) * SUM_ROWS)
        acc = got[0, part, :].astype(F32)
        for n in range(1, NEAR):
            acc = acc + got[n, part, :].astype(F32)
        tail = jnp.sum(jnp.where(slot == far, tails, 0.0), axis=0, keepdims=True)
        out[far, 0:SUM_ROWS, :] = acc.astype(BF16)
        out[far, SUM_ROWS:PAY, :] = split(tail + pltpu.roll(tail, ROWS, 1), front)


def far_kernel(got, out, sent):
    front = lax.broadcasted_iota(jnp.int32, (1, 128), 1) < ROWS
    acc = got[0].astype(F32)
    for f in range(1, FAR):
        acc = acc + got[f].astype(F32)
    total = acc[0:SUM_ROWS]
    tail = acc[SUM_ROWS:PAY, :]
    mass = tail + pltpu.roll(tail, ROWS, 1)
    out[0:SUM_ROWS, :] = total
    out[SUM_ROWS:PAY, :] = mass
    sent[0:SUM_ROWS, :] = total.astype(BF16)
    sent[SUM_ROWS:PAY, :] = split(mass[0:1], front)


def final_kernel(own, one, two, three, centers, prior, out, held, sem):
    lane_at = lax.axis_index("lane")
    copy = pltpu.make_async_copy(
        centers.at[0, pl.ds(pl.multiple_of(lane_at * ROWS, ROWS), ROWS)], held, sem
    )
    copy.start()
    past = one[...].astype(F32) + two[...].astype(F32) + three[...].astype(F32)
    acc = own[0:SUM_ROWS, :] + past[0:SUM_ROWS]
    tail = past[SUM_ROWS : SUM_ROWS + 1, :]
    mass = own[SUM_ROWS : SUM_ROWS + 1, :] + tail + pltpu.roll(tail, ROWS, 1)
    row = lax.broadcasted_iota(jnp.int32, (ROWS, ROWS), 0)
    lane = lax.broadcasted_iota(jnp.int32, (ROWS, ROWS), 1)
    pick = row == lane

    def column(value):
        wide = jnp.broadcast_to(value, (ROWS, ROWS))
        return jnp.sum(jnp.where(pick, wide, 0.0), axis=1, keepdims=True)

    weight = column(prior[...])
    inverse = 1.0 / (weight + column(mass[:, 0:ROWS]))
    copy.wait()
    for c in range(3):
        numer = weight * held[:, c * 128 : (c + 1) * 128].astype(F32) + acc[
            c * ROWS : (c + 1) * ROWS, :
        ]
        out[0, 0, :, c * 128 : (c + 1) * 128] = numer * inverse


def per_device(raw, taps, whitening, basis, project, centroids, prior, times, counts):
    windows = ("section", "lane")
    count = SECTIONS * LANES
    head, tail = call(
        edges_kernel,
        (jax.ShapeDtypeStruct((AFTER, CH), BF16), jax.ShapeDtypeStruct((BEFORE, CH), BF16)),
        [VMEM],
        (VMEM, VMEM),
        moved=1_000_000,
    )(raw)
    before = lax.ppermute(tail, windows, [(i, i + 1) for i in range(count - 1)])
    after = lax.ppermute(head, windows, [(i + 1, i) for i in range(count - 1)])
    held = inner(raw, taps.reshape(1, TAPS), whitening, basis.T, times)
    feats = features(before, after, raw, whitening, *held, project)
    spikes = lax.all_gather(feats, "group", axis=0, tiled=True)
    shares, weights, tops = scores(spikes, centroids, counts)
    shares = lax.all_to_all(shares, "group", 0, 0)
    parts = sums(shares, weights, tops, spikes)
    near = [[NEAR * far + n for n in range(NEAR)] for far in range(FAR)]
    got = lax.all_to_all(parts, "lane", 0, 0, axis_index_groups=near)
    small = jax.ShapeDtypeStruct((PAY, 128), BF16)
    wide = jax.ShapeDtypeStruct((PAY, 128), F32)
    far = [[NEAR * f + n for f in range(FAR)] for n in range(NEAR)]
    block = jax.ShapeDtypeStruct((FAR, PAY, 128), BF16)
    halves = call(near_kernel, block, [VMEM], VMEM, moved=1_000_000)(got)
    halves = lax.all_to_all(halves, "lane", 0, 0, axis_index_groups=far)
    total, sent = call(far_kernel, (wide, small), [VMEM], (VMEM,) * 2, moved=300_000)(halves)
    earlier = [
        lax.ppermute(sent, "section", [(i, i + d) for i in range(SECTIONS - d)])
        for d in range(1, SECTIONS)
    ]
    return call(
        final_kernel,
        jax.ShapeDtypeStruct((1, 1, ROWS, FEAT), F32),
        [VMEM, VMEM, VMEM, VMEM, ANY, VMEM],
        VMEM,
        [pltpu.VMEM((ROWS, FEAT), BF16), pltpu.SemaphoreType.DMA],
        moved=600_000,
    )(total, *earlier, centroids, prior)


def solution(mesh):
    placed = (
        P(("section", "lane"), "group"),
        P(),
        P("group", None),
        P(),
        P(),
        P("group", None, None),
        P("group", "lane"),
        P(("section", "lane"), "group", None),
        P(("section", "lane"), "group"),
    )
    return jax.shard_map(
        per_device,
        mesh=mesh,
        in_specs=placed,
        out_specs=P("section", "group", "lane", None),
        check_vma=False,
    )
```
